256 devices in a mesh: grp: 8 (over y, core), dev: 32 (over z, x).
Axes of the slice: x: 4, y: 4, z: 8, core: 2. Of those that a mesh axis runs over, the one named last changes fastest.
Arguments:
- cell_state: float32 [258, 65536], P(None, ('grp', 'dev')), may hold values from 0.5 to 2, as said below
- stiff_flags: int32 [65536], P(('grp', 'dev')), may hold values from 0 to 1, as said below
- reactants: int32 [2, 1548], replicated, may hold values from 0 to 256, as said below
- collision_frequency_multipliers: float32 [1548], replicated, may hold values from 0.5 to 1.5
- barrier_energies: float32 [1548], replicated, may hold values from 0 to 1
- stoichiometry: float32 [258, 1548], replicated, may hold values from -1 to 1, as said below
- face_cells: int32 [2, 32768], P(None, ('grp', 'dev')), may hold values from 0 to 255
Outputs:
- advanced: float32 [258, 65536], P(None, ('grp', 'dev'))
- face_jump: float32 [258, 2, 32768], P(None, None, ('grp', 'dev'))
The draws below stay inside these ranges and needn't reach their ends.
Inputs may be any that keep to these rules, and one draw needn't show every extreme that they name: `stiff_flags`: exactly 128 times the number of devices cells are stiff in all; in every draw one device has all 256 of its cells stiff and another none. Both reactants of reaction j lie in block j // 36, that is among components 6 * (j // 36) to 6 * (j // 36) + 5, and are never the temperature, component 258 - 1. `cell_state`: components 0 to 256 lie in [0.5, 1]; component 258 - 1 lies in [1, 2]. `stoichiometry`: every entry has magnitude 0.5 to 1.
All inputs are finite; a program needn't handle non-finite values.
Results may differ from the reference program's by a relative error of at most 0.00023.
Values sent between devices are 32-bit elements; how exact they have to be, the bound alone decides.
A program may use at most 64 MiB of HBM per device.

```python
import math
import jax
import jax.numpy as jnp
from jax import lax

NB = 43
BS = 6
SPEC = 258
RPB = 36
NR = 1548
C_DEV = 256
F_DEV = 128
LOAD = 128
TOTAL_BURN_ZONES = 65536
FACES = 32768
N_GRP = 8
N_DEV = 32


def draw_cell_state(key, part):
    key = jax.random.fold_in(key, 5)
    first_key, successor_seed = jax.random.split(key)
    mixture_constituents = jax.random.uniform(first_key, (SPEC - 1, TOTAL_BURN_ZONES), jnp.float32)
    zone_thermal_level = jax.random.uniform(successor_seed, (1, TOTAL_BURN_ZONES), jnp.float32)
    return jnp.concatenate([0.5 + 0.5 * mixture_constituents, 1.0 + zone_thermal_level], axis=0)


def draw_stoichiometry(key, part):
    key = jax.random.fold_in(key, 7)
    first_key, successor_seed = jax.random.split(key)
    sign_draw = jax.random.uniform(first_key, (SPEC, NR), jnp.float32)
    size_factor = jax.random.uniform(successor_seed, (SPEC, NR), jnp.float32)
    return jnp.where(sign_draw < 0.5, -1.0, 1.0) * (0.5 + 0.5 * size_factor)


def draw_reactants(key, part):
    key = jax.random.fold_in(key, 11)
    first_key, successor_seed = jax.random.split(key)
    block_of = jnp.arange(NR, dtype=jnp.int32) // RPB
    wide_pick = jax.random.randint(first_key, (2, NR), 0, BS, dtype=jnp.int32)
    narrow_pick = jax.random.randint(successor_seed, (2, NR), 0, BS - 1, dtype=jnp.int32)
    offset = jnp.where(block_of[None, :] == NB - 1, narrow_pick, wide_pick)
    return (block_of[None, :] * BS + offset).astype(jnp.int32)


def draw_stiff_flags(key, part):
    key = jax.random.fold_in(key, 13)
    processor_count = TOTAL_BURN_ZONES // C_DEV
    half_count = processor_count // 2
    excess_key, forced_key, order_key, sign_key, mask_key = jax.random.split(key, 5)
    excess = jax.random.randint(excess_key, (half_count,), -LOAD, LOAD + 1, dtype=jnp.int32)
    forced = jax.random.randint(forced_key, (), 0, half_count, dtype=jnp.int32)
    sign_flip = 2 * jax.random.randint(sign_key, (), 0, 2, dtype=jnp.int32) - 1
    excess = jnp.where(jnp.arange(half_count, dtype=jnp.int32) == forced, sign_flip * LOAD, excess)
    counts = jnp.concatenate([LOAD + excess, LOAD - excess])
    counts = counts[jax.random.permutation(order_key, processor_count)]
    subkeys = jax.random.split(mask_key, processor_count)
    ranking = jax.vmap(lambda subkey: jax.random.permutation(subkey, C_DEV))(subkeys)
    return (ranking < counts[:, None]).astype(jnp.int32).reshape(TOTAL_BURN_ZONES)


def with_ends(drawn, stream_key, smallest, top_value):
    index_at = [jax.random.randint(jax.random.fold_in(stream_key, axis), (), 0, length) for axis, length in enumerate(drawn.shape)]
    longest = drawn.shape.index(max(drawn.shape))
    neighbour = index_at[:longest] + [(index_at[longest] + 1) % drawn.shape[longest]] + index_at[longest + 1:]
    return drawn.at[tuple(index_at)].set(smallest).at[tuple(neighbour)].set(top_value)


def setup_inputs(seed: int = 0) -> dict:
    seeds = jax.random.split(jax.random.key(seed), 8)
    return {
        "cell_state": draw_cell_state(jax.random.fold_in(seeds[7], 71), 0),
        "stiff_flags": draw_stiff_flags(jax.random.fold_in(seeds[7], 71), 0),
        "reactants": draw_reactants(jax.random.fold_in(seeds[7], 71), 0),
        "collision_frequency_multipliers": jnp.clip(jnp.exp(jax.random.uniform(seeds[3], (NR,), jnp.float32, math.log(0.5), math.log(1.5))), 0.5, 1.5),
        "barrier_energies": jnp.clip(jax.random.uniform(seeds[4], (NR,), jnp.float32, 0.0, 1.0), 0.0, 1.0),
        "stoichiometry": draw_stoichiometry(jax.random.fold_in(seeds[7], 71), 0),
        "face_cells": with_ends(jax.random.randint(seeds[6], (2, FACES), 0, C_DEV), jax.random.fold_in(seeds[6], 1), 0, C_DEV - 1).astype(jnp.int32),
    }


TIME_STEP = 0.01
SECTION_GAMMA = 0.5
SECTION_A = (2.0, 1.867943637803922, 0.2344449711399156)
SECTION_C = (-7.137615036412310, 2.580708087951457, 0.6515950076447975, -2.137148994382534, -0.3214669691237626, -0.6949742501781779)
SECTION_M = (2.255570073418735, 0.2870493262186792, 0.4353179431840180, 1.093502252409163)


def reaction_speed_constants(zone_thermal_level, collision_frequency_multipliers, barrier_energies):
    return collision_frequency_multipliers[:, None] * jnp.exp(barrier_energies[:, None] * (1.0 - 1.0 / zone_thermal_level[None, :]))


def mass_action(cell_state, reactants, coefficients):
    former = jnp.take(cell_state, reactants[0], axis=0)
    latter = jnp.take(cell_state, reactants[1], axis=0)
    return coefficients * former * latter


def source_term(stoichiometry, reaction_rates):
    return jnp.dot(stoichiometry, reaction_rates, precision=lax.Precision.HIGHEST, preferred_element_type=jnp.float32)


def explicit_step(cell_state, reactants, collision_frequency_multipliers, barrier_energies, stoichiometry):
    coefficients = reaction_speed_constants(cell_state[-1], collision_frequency_multipliers, barrier_energies)
    return cell_state + TIME_STEP * source_term(stoichiometry, mass_action(cell_state, reactants, coefficients))


def block_coupling(stoichiometry, reactants):
    shaped = stoichiometry.reshape(NB, BS, NB, RPB)
    blocks = jnp.transpose(jnp.diagonal(shaped, axis1=0, axis2=2), (2, 0, 1))
    offsets = reactants.reshape(2, NB, RPB) - (jnp.arange(NB, dtype=jnp.int32) * BS)[None, :, None]
    select = (offsets[..., None] == jnp.arange(BS, dtype=jnp.int32)[None, None, None, :]).astype(jnp.float32)
    by_first = blocks[:, :, None, :] * jnp.transpose(select[0], (0, 2, 1))[:, None, :, :]
    by_second = blocks[:, :, None, :] * jnp.transpose(select[1], (0, 2, 1))[:, None, :, :]
    return jnp.concatenate([by_first, by_second], axis=3).reshape(NB, BS * BS, 2 * RPB)


def factor_blocks(system):
    shaped = system.reshape(NB, BS, BS, -1)
    entries = [[shaped[:, target, column] for column in range(BS)] for target in range(BS)]
    inverses = []
    for pivot_at in range(BS):
        inverse = 1.0 / entries[pivot_at][pivot_at]
        inverses.append(inverse)
        for target in range(pivot_at + 1, BS):
            entries[target][pivot_at] = entries[target][pivot_at] * inverse
            for column in range(pivot_at + 1, BS):
                entries[target][column] = entries[target][column] - entries[target][pivot_at] * entries[pivot_at][column]
    return entries, inverses


def solve_blocks(entries, inverses, right_side):
    blocked = right_side.reshape(NB, BS, -1)
    solution = [blocked[:, target] for target in range(BS)]
    for target in range(BS):
        for column in range(target):
            solution[target] = solution[target] - entries[target][column] * solution[column]
    for target in reversed(range(BS)):
        for column in range(target + 1, BS):
            solution[target] = solution[target] - entries[target][column] * solution[column]
        solution[target] = solution[target] * inverses[target]
    return jnp.stack(solution, axis=1).reshape(NB * BS, -1)


def integrate(cell_state, reactants, collision_frequency_multipliers, barrier_energies, stoichiometry, coupling):
    column_count = cell_state.shape[1]
    coefficients = reaction_speed_constants(cell_state[-1], collision_frequency_multipliers, barrier_energies)
    former = jnp.take(cell_state, reactants[0], axis=0)
    latter = jnp.take(cell_state, reactants[1], axis=0)
    initial = source_term(stoichiometry, coefficients * former * latter)
    factors = jnp.concatenate([(coefficients * latter).reshape(NB, RPB, column_count), (coefficients * former).reshape(NB, RPB, column_count)], axis=1)
    jacobian = jnp.einsum("bkj,bjn->bkn", coupling, factors, precision=lax.Precision.HIGHEST)
    scaled = TIME_STEP * SECTION_GAMMA
    identity = jnp.eye(BS, dtype=jnp.float32).reshape(1, BS * BS, 1)
    entries, inverses = factor_blocks(identity - scaled * jacobian)
    section_one = solve_blocks(entries, inverses, scaled * initial)
    second_state = cell_state + SECTION_A[0] * section_one
    second_rate = source_term(stoichiometry, mass_action(second_state, reactants, coefficients))
    section_two = solve_blocks(entries, inverses, scaled * second_rate + SECTION_GAMMA * SECTION_C[0] * section_one)
    third_state = cell_state + SECTION_A[1] * section_one + SECTION_A[2] * section_two
    third_rate = source_term(stoichiometry, mass_action(third_state, reactants, coefficients))
    section_three = solve_blocks(entries, inverses, scaled * third_rate + SECTION_GAMMA * (SECTION_C[1] * section_one + SECTION_C[2] * section_two))
    section_four = solve_blocks(entries, inverses, scaled * third_rate + SECTION_GAMMA * (SECTION_C[3] * section_one + SECTION_C[4] * section_two + SECTION_C[5] * section_three))
    return cell_state + SECTION_M[0] * section_one + SECTION_M[1] * section_two + SECTION_M[2] * section_three + SECTION_M[3] * section_four


def reference(cell_state, stiff_flags, reactants, collision_frequency_multipliers, barrier_energies, stoichiometry, face_cells):
    processor_count = N_GRP * N_DEV
    coupling = block_coupling(stoichiometry, reactants)
    per_device = jnp.transpose(cell_state.reshape(SPEC, processor_count, C_DEV), (1, 0, 2))

    def explicit_one(block_state):
        return explicit_step(block_state, reactants, collision_frequency_multipliers, barrier_energies, stoichiometry)

    explicit = lax.map(explicit_one, per_device)
    explicit = jnp.transpose(explicit, (1, 0, 2)).reshape(SPEC, TOTAL_BURN_ZONES)
    picked = jnp.nonzero(stiff_flags, size=processor_count * LOAD, fill_value=0)[0].astype(jnp.int32)
    chosen = jnp.transpose(jnp.take(cell_state, picked, axis=1).reshape(SPEC, processor_count, LOAD), (1, 0, 2))

    def implicit_one(block_state):
        return integrate(block_state, reactants, collision_frequency_multipliers, barrier_energies, stoichiometry, coupling)

    solved = lax.map(implicit_one, chosen)
    solved = jnp.transpose(solved, (1, 0, 2)).reshape(SPEC, processor_count * LOAD)
    advanced = explicit.at[:, picked].set(solved)
    owner_start = ((jnp.arange(FACES, dtype=jnp.int32) // F_DEV) * C_DEV).astype(jnp.int32)
    face_index = (face_cells + owner_start[None, :]).astype(jnp.int32)
    face_states = jnp.take(advanced, face_index, axis=1)
    face_grid = face_states.reshape(SPEC, 2, N_GRP, N_DEV, F_DEV)
    boundary = jnp.zeros((SPEC, N_GRP, 1, F_DEV), jnp.float32)
    from_below = jnp.concatenate([boundary, face_grid[:, 1, :, :-1]], axis=2)
    from_above = jnp.concatenate([face_grid[:, 0, :, 1:], boundary], axis=2)
    face_jump = jnp.stack([from_below - face_grid[:, 0], from_above - face_grid[:, 1]], axis=1).reshape(SPEC, 2, FACES)
    return advanced, face_jump
```

```python
import jax
import jax.numpy as jnp
from jax import lax
from jax.experimental import pallas as pl
from jax.experimental.pallas import tpu as pltpu
from jax.sharding import PartitionSpec as P

NB = 43
BS = 6
RPB = 36
SPEC = 258
NR = 1548
CELLS = 256
FACES = 128

GROUP = 8
GROUPS = 6
GROUP_STATE = GROUP * BS
GROUP_RATES = GROUP * RPB
STATE_ROWS = GROUPS * GROUP_STATE
LAST_RATES = 112
RATE_ROWS = 1664
CHUNK = 96
S_ROWS = 272

TIME_STEP = 0.01
GAMMA = 0.5
SCALED = TIME_STEP * GAMMA
A = (2.0, 1.867943637803922, 0.2344449711399156)
C = (
    -7.13761503641231,
    2.580708087951457,
    0.6515950076447975,
    -2.137148994382534,
    -0.3214669691237626,
    -0.6949742501781779,
)
M = (2.255570073418735, 0.2870493262186792, 0.435317943184018, 1.093502252409163)

BF = jnp.bfloat16
F32 = jnp.float32


def dot(a, b):
    return jnp.dot(a, b, preferred_element_type=F32)


def split2(x):
    hi = x.astype(BF)
    return hi, (x - hi.astype(F32)).astype(BF)


def split3(x):
    hi = x.astype(BF)
    rest = x - hi.astype(F32)
    mid = rest.astype(BF)
    return hi, mid, (rest - mid.astype(F32)).astype(BF)


def chunks_of(group):
    start = group * GROUP_RATES
    if group == GROUPS - 1:
        return [(start, LAST_RATES)]
    return [(start + k, CHUNK) for k in range(0, GROUP_RATES, CHUNK)]


def window_of(group):
    start = group * GROUP_RATES // 128 * 128
    return start, (256 if group == GROUPS - 1 else 384)


def factor(e):
    for p in range(BS):
        inverse = 1.0 / e[p][p]
        e[p][p] = inverse
        for t in range(p + 1, BS):
            e[t][p] = e[t][p] * inverse
            for c in range(p + 1, BS):
                e[t][c] = e[t][c] - e[t][p] * e[p][c]
    return e


def solve(e, b):
    x = list(b)
    for t in range(BS):
        for c in range(t):
            x[t] = x[t] - e[t][c] * x[c]
    for t in reversed(range(BS)):
        for c in range(t + 1, BS):
            x[t] = x[t] - e[t][c] * x[c]
        x[t] = x[t] * e[t][t]
    return x


def kernel(
    state_ref,
    flags_ref,
    reactants_ref,
    frequency_ref,
    barrier_ref,
    stoich_ref,
    faces_ref,
    advanced_ref,
    face_ref,
    rows,
    columns,
    s_hi,
    s_lo,
    s_tile,
    y_half,
    src_half,
    y0,
    gather,
    y_split,
    coef,
    r_hi,
    r_lo,
    fac,
    coupling,
    lu,
    explicit,
    u1,
    u2,
):
    rows[...] = jnp.zeros_like(rows)
    rows[:, 1536:] = jnp.where(
        lax.broadcasted_iota(jnp.int32, (8, 128), 0) >= 2, -1.0, 0.0
    )
    rows[0:1, :NR] = frequency_ref[...]
    rows[1:2, :NR] = barrier_ref[...]
    reactants = reactants_ref[...]
    lane = lax.broadcasted_iota(jnp.int32, (2, NR), 1)
    first = jnp.zeros((2, NR), jnp.int32)
    for g in range(1, GROUPS):
        first = jnp.where(lane >= g * GROUP_RATES, g * GROUP_STATE, first)
    local = reactants - first
    block = (local * 43) >> 8
    slot = (local - block * BS) * GROUP + block
    rows[2:4, :NR] = slot.astype(F32)
    rows[4:6, :NR] = reactants.astype(F32)
    columns[...] = jnp.transpose(rows[...])

    y_half[:, SPEC // 8 * 8 :, :] = jnp.zeros((2, STATE_ROWS - SPEC // 8 * 8, 128), F32)
    src_half[:, SPEC // 8 * 8 :, :] = jnp.zeros((2, STATE_ROWS - SPEC // 8 * 8, 128), F32)
    for h in range(2):
        y_half[h, :SPEC, :] = state_ref[:, h * 128 : (h + 1) * 128]
    s_hi[:, 1536:] = jnp.zeros((S_ROWS, 128), BF)
    s_lo[:, 1536:] = jnp.zeros((S_ROWS, 128), BF)
    s_hi[256:, :] = jnp.zeros((S_ROWS - 256, RATE_ROWS), BF)
    s_lo[256:, :] = jnp.zeros((S_ROWS - 256, RATE_ROWS), BF)
    for at in range(0, SPEC, 16):
        n = min(16, SPEC - at)
        hi, lo = split2(stoich_ref[at : at + n, :])
        s_hi[at : at + n, :NR] = hi
        s_lo[at : at + n, :NR] = lo

    for g in range(GROUPS):
        for start, n in chunks_of(g):
            spot = lax.rem(lax.broadcasted_iota(jnp.int32, (n, 3 * GROUP_STATE), 1), GROUP_STATE)
            for which in range(2):
                want = columns[start : start + n, 2 + which : 3 + which].astype(jnp.int32)
                hot = (want == spot).astype(F32).astype(BF)
                gather[which, start : start + n, :] = hot

    def spread(ref, g, h):
        return [ref[h, pl.ds(g * GROUP_STATE + m, GROUP, stride=BS), :] for m in range(BS)]

    def pieces(ref, g, h):
        at = g * GROUP_STATE
        lanes = slice(h * 128, (h + 1) * 128)
        return [ref[at + m * GROUP : at + (m + 1) * GROUP, lanes] for m in range(BS)]

    def put(ref, g, h, values):
        at = g * GROUP_STATE
        lanes = slice(h * 128, (h + 1) * 128)
        for m in range(BS):
            ref[at + m * GROUP : at + (m + 1) * GROUP, lanes] = values[m]

    def put_state(g, parts):
        for k, part in enumerate(split3(parts)):
            at = g * 3 * GROUP_STATE + k * GROUP_STATE
            y_split[at : at + GROUP_STATE, :] = part

    def reactant(which, g, start, n):
        at = g * 3 * GROUP_STATE
        return dot(gather[which, start : start + n, :], y_split[at : at + 3 * GROUP_STATE, :])

    r_hi[NR // 16 * 16 :, :] = jnp.zeros((RATE_ROWS - NR // 16 * 16, CELLS), BF)
    r_lo[NR // 16 * 16 :, :] = jnp.zeros((RATE_ROWS - NR // 16 * 16, CELLS), BF)
    fac[:, NR // 16 * 16 :, :] = jnp.zeros((2, RATE_ROWS - NR // 16 * 16, CELLS), BF)

    theta = 1.0 - 1.0 / state_ref[SPEC - 1 : SPEC, :]
    for g in range(GROUPS):
        for h in range(2):
            put(y0, g, h, spread(y_half, g, h))
        put_state(g, y0[g * GROUP_STATE : (g + 1) * GROUP_STATE, :])
        for start, n in chunks_of(g):
            k = columns[start : start + n, 0:1] * jnp.exp(columns[start : start + n, 1:2] * theta)
            coef[start : start + n, :] = k
            former = reactant(0, g, start, n)
            latter = reactant(1, g, start, n)
            by_first = k * latter
            fac[0, start : start + n, :] = by_first.astype(BF)
            fac[1, start : start + n, :] = (k * former).astype(BF)
            hi, lo = split2(by_first * former)
            r_hi[start : start + n, :] = hi
            r_lo[start : start + n, :] = lo

    def source_term():
        total = (
            dot(s_hi[...], r_hi[...]) + dot(s_lo[...], r_hi[...]) + dot(s_hi[...], r_lo[...])
        )
        for h in range(2):
            src_half[h, :S_ROWS, :] = total[:, h * 128 : (h + 1) * 128]

    def rates():
        for g in range(GROUPS):
            for start, n in chunks_of(g):
                k = coef[start : start + n, :]
                hi, lo = split2(k * reactant(0, g, start, n) * reactant(1, g, start, n))
                r_hi[start : start + n, :] = hi
                r_lo[start : start + n, :] = lo

    source_term()

    sub = lax.broadcasted_iota(jnp.int32, (GROUP, 1), 0) * BS
    for g in range(GROUPS):
        w, width = window_of(g)
        rows_here = min(GROUP_STATE, SPEC - g * GROUP_STATE)
        if rows_here < GROUP_STATE:
            s_tile[...] = jnp.zeros_like(s_tile)
        for t in range(0, width, 128):
            last = min(128, NR - w - t)
            if last > 0:
                s_tile[t // 128, :rows_here, :last] = stoich_ref[
                    g * GROUP_STATE : g * GROUP_STATE + rows_here, w + t : w + t + last
                ]
        slabs = [
            [s_tile[t, pl.ds(i, GROUP, stride=BS), :] for t in range(width // 128)]
            for i in range(BS)
        ]
        for which in range(2):
            reacts = rows[4 + which : 5 + which, w : w + width].astype(jnp.int32)
            masks = [reacts == sub + (g * GROUP_STATE + m) for m in range(BS)]
            for i in range(BS):
                s = jnp.concatenate(slabs[i], axis=1)
                for m in range(0, BS, 2):
                    pair = jnp.concatenate(
                        [jnp.where(masks[m], s, 0.0), jnp.where(masks[m + 1], s, 0.0)], axis=0
                    )
                    to = (i * BS + m) * GROUP
                    coupling[to : to + 16, which * width : (which + 1) * width] = pair.astype(BF)
        jacobian = dot(coupling[:, :width], fac[0, w : w + width, :]) + dot(
            coupling[:, width : 2 * width], fac[1, w : w + width, :]
        )
        lu[g, :, :] = jacobian

    def put_split(g, h, values):
        lanes = slice(h * 128, (h + 1) * 128)
        at = g * 3 * GROUP_STATE
        for m in range(0, BS, 2):
            both = jnp.concatenate([values[m], values[m + 1]], axis=0)
            for k, part in enumerate(split3(both)):
                to = at + k * GROUP_STATE + m * GROUP
                y_split[to : to + 16, lanes] = part

    def factors(g, h):
        lanes = slice(h * 128, (h + 1) * 128)
        return [
            [
                lu[g, (i * BS + m) * GROUP : (i * BS + m + 1) * GROUP, lanes]
                for m in range(BS)
            ]
            for i in range(BS)
        ]

    for g in range(GROUPS):
        for h in range(2):
            lanes = slice(h * 128, (h + 1) * 128)
            e = factors(g, h)
            e = [
                [(1.0 if i == m else 0.0) - SCALED * e[i][m] for m in range(BS)]
                for i in range(BS)
            ]
            e = factor(e)
            for i in range(BS):
                for m in range(BS):
                    lu[g, (i * BS + m) * GROUP : (i * BS + m + 1) * GROUP, lanes] = e[i][m]
            x = solve(e, [SCALED * s for s in spread(src_half, g, h)])
            put(u1, g, h, x)
            put_split(g, h, [y + A[0] * u for y, u in zip(pieces(y0, g, h), x)])
            y = pieces(y0, g, h)
            s = spread(src_half, g, h)
            put(explicit, g, h, [a + TIME_STEP * b for a, b in zip(y, s)])

    rates()
    source_term()
    for g in range(GROUPS):
        for h in range(2):
            e = factors(g, h)
            one = pieces(u1, g, h)
            x = solve(
                e, [SCALED * s + (GAMMA * C[0]) * u for s, u in zip(spread(src_half, g, h), one)]
            )
            put(u2, g, h, x)
            put_split(
                g,
                h,
                [y + A[1] * a + A[2] * b for y, a, b in zip(pieces(y0, g, h), one, x)],
            )

    rates()
    source_term()
    hot = jnp.concatenate(
        [
            lax.broadcasted_iota(jnp.int32, (CELLS, FACES), 0) == faces_ref[0:1, :],
            lax.broadcasted_iota(jnp.int32, (CELLS, FACES), 0) == faces_ref[1:2, :],
        ],
        axis=1,
    )
    hot = hot.astype(F32).astype(BF)
    for g in range(GROUPS):
        for h in range(2):
            lanes = slice(h * 128, (h + 1) * 128)
            e = factors(g, h)
            one = pieces(u1, g, h)
            two = pieces(u2, g, h)
            base = [SCALED * s for s in spread(src_half, g, h)]
            three = solve(
                e,
                [
                    s + (GAMMA * C[1]) * a + (GAMMA * C[2]) * b
                    for s, a, b in zip(base, one, two)
                ],
            )
            four = solve(
                e,
                [
                    s + (GAMMA * C[3]) * a + (GAMMA * C[4]) * b + (GAMMA * C[5]) * c
                    for s, a, b, c in zip(base, one, two, three)
                ],
            )
            stiff = flags_ref[0:1, lanes] == 1
            out = [
                jnp.where(stiff, y + M[0] * a + M[1] * b + M[2] * c + M[3] * d, x)
                for y, a, b, c, d, x in zip(
                    pieces(y0, g, h), one, two, three, four, pieces(explicit, g, h)
                )
            ]
            for m in range(BS):
                y_half[h, pl.ds(g * GROUP_STATE + m, GROUP, stride=BS), :] = out[m]
        count = min(GROUP_STATE, SPEC - g * GROUP_STATE)
        here = slice(g * GROUP_STATE, g * GROUP_STATE + GROUP_STATE)
        real = slice(g * GROUP_STATE, g * GROUP_STATE + count)
        done = jnp.concatenate([y_half[0, here, :], y_half[1, here, :]], axis=1)
        advanced_ref[real, :] = done[:count]
        face = sum(dot(part, hot) for part in split3(done))
        face_ref[real, :] = face[:count]


def compute(state, flags, reactants, frequency, barrier, stoich, faces):
    return pl.pallas_call(
        kernel,
        out_shape=(
            jax.ShapeDtypeStruct((SPEC, CELLS), F32),
            jax.ShapeDtypeStruct((SPEC, 2 * FACES), F32),
        ),
        in_specs=[pl.BlockSpec(memory_space=pltpu.VMEM)] * 7,
        out_specs=[pl.BlockSpec(memory_space=pltpu.VMEM)] * 2,
        scratch_shapes=[
            pltpu.VMEM((8, RATE_ROWS), F32),
            pltpu.VMEM((RATE_ROWS, 8), F32),
            pltpu.VMEM((S_ROWS, RATE_ROWS), BF),
            pltpu.VMEM((S_ROWS, RATE_ROWS), BF),
            pltpu.VMEM((3, GROUP_STATE, 128), F32),
            pltpu.VMEM((2, STATE_ROWS, 128), F32),
            pltpu.VMEM((2, STATE_ROWS, 128), F32),
            pltpu.VMEM((STATE_ROWS, CELLS), F32),
            pltpu.VMEM((2, RATE_ROWS, 3 * GROUP_STATE), BF),
            pltpu.VMEM((3 * STATE_ROWS, CELLS), BF),
            pltpu.VMEM((RATE_ROWS, CELLS), F32),
            pltpu.VMEM((RATE_ROWS, CELLS), BF),
            pltpu.VMEM((RATE_ROWS, CELLS), BF),
            pltpu.VMEM((2, RATE_ROWS, CELLS), BF),
            pltpu.VMEM((STATE_ROWS, 768), BF),
            pltpu.VMEM((GROUPS, STATE_ROWS, CELLS), F32),
            pltpu.VMEM((STATE_ROWS, CELLS), F32),
            pltpu.VMEM((STATE_ROWS, CELLS), F32),
            pltpu.VMEM((STATE_ROWS, CELLS), F32),
        ],
        compiler_params=pltpu.CompilerParams(vmem_limit_bytes=48 * 1024 * 1024),
        cost_estimate=pl.CostEstimate(
            flops=4_000_000_000, bytes_accessed=3_000_000, transcendentals=400_000
        ),
    )(
        state,
        flags.reshape(1, CELLS),
        reactants,
        frequency.reshape(1, NR),
        barrier.reshape(1, NR),
        stoich,
        faces,
    )


def on_device(state, flags, reactants, frequency, barrier, stoich, faces):
    advanced, face = compute(state, flags, reactants, frequency, barrier, stoich, faces)
    lower, upper = face[:, :FACES], face[:, FACES:]
    size = lax.axis_size("dev")
    up = [(i, i + 1) for i in range(size - 1)]
    down = [(i + 1, i) for i in range(size - 1)]
    before = lax.ppermute(upper, "dev", up)
    after = lax.ppermute(lower, "dev", down)
    return advanced, jnp.stack([before - lower, after - upper], axis=1)


def solution(mesh):
    cells = P(None, ("grp", "dev"))
    return jax.shard_map(
        on_device,
        mesh=mesh,
        in_specs=(cells, P(("grp", "dev")), P(), P(), P(), P(), cells),
        out_specs=(cells, P(None, None, ("grp", "dev"))),
        check_vma=False,
    )
```

```python
import jax
import jax.numpy as jnp
from jax import lax
from jax.experimental import pallas as pl
from jax.experimental.pallas import tpu as pltpu
from jax.sharding import PartitionSpec as P

NB = 43
BS = 6
RPB = 36
SPEC = 258
NR = 1548
CELLS = 256
FACES = 128

GROUP = 8
GROUPS = 6
GROUP_STATE = GROUP * BS
GROUP_RATES = GROUP * RPB
STATE_ROWS = GROUPS * GROUP_STATE
LAST_RATES = 112
RATE_ROWS = 1664
CHUNK = 96
S_ROWS = 272

TIME_STEP = 0.01
GAMMA = 0.5
SCALED = TIME_STEP * GAMMA
A = (2.0, 1.867943637803922, 0.2344449711399156)
C = (
    -7.13761503641231,
    2.580708087951457,
    0.6515950076447975,
    -2.137148994382534,
    -0.3214669691237626,
    -0.6949742501781779,
)
M = (2.255570073418735, 0.2870493262186792, 0.435317943184018, 1.093502252409163)

BF = jnp.bfloat16
F32 = jnp.float32


def dot(a, b):
    return jnp.dot(a, b, preferred_element_type=F32)


def split2(x):
    hi = x.astype(BF)
    return hi, (x - hi.astype(F32)).astype(BF)


def split3(x):
    hi = x.astype(BF)
    rest = x - hi.astype(F32)
    mid = rest.astype(BF)
    return hi, mid, (rest - mid.astype(F32)).astype(BF)


def chunks_of(group):
    start = group * GROUP_RATES
    if group == GROUPS - 1:
        return [(start, LAST_RATES)]
    return [(start + k, CHUNK) for k in range(0, GROUP_RATES, CHUNK)]


def window_of(group):
    start = group * GROUP_RATES // 128 * 128
    return start, (256 if group == GROUPS - 1 else 384)


def factor(e):
    for p in range(BS):
        inverse = 1.0 / e[p][p]
        e[p][p] = inverse
        for t in range(p + 1, BS):
            e[t][p] = e[t][p] * inverse
            for c in range(p + 1, BS):
                e[t][c] = e[t][c] - e[t][p] * e[p][c]
    return e


def solve(e, b):
    x = list(b)
    for t in range(BS):
        for c in range(t):
            x[t] = x[t] - e[t][c] * x[c]
    for t in reversed(range(BS)):
        for c in range(t + 1, BS):
            x[t] = x[t] - e[t][c] * x[c]
        x[t] = x[t] * e[t][t]
    return x


def kernel(
    state_hbm,
    flags_hbm,
    reactants_hbm,
    frequency_hbm,
    barrier_hbm,
    stoich_hbm,
    faces_hbm,
    advanced_ref,
    jump_ref,
    state_ref,
    flags_ref,
    reactants_ref,
    frequency_ref,
    barrier_ref,
    stoich_ref,
    faces_ref,
    in_sem,
    face,
    received,
    send_sem,
    recv_sem,
    rows,
    columns,
    s_hi,
    s_lo,
    s_tile,
    y_half,
    src_half,
    y0,
    gather,
    y_split,
    coef,
    r_hi,
    r_lo,
    fac,
    coupling,
    lu,
    explicit,
    u1,
    u2,
):
    me = lax.axis_index("dev")
    count = lax.axis_size("dev")
    up = lax.rem(me + 1, count)
    down = lax.rem(me + count - 1, count)
    barrier = pltpu.get_barrier_semaphore()
    for other in (up, down):
        pl.semaphore_signal(
            barrier, inc=1, device_id={"dev": other}, device_id_type=pl.DeviceIdType.MESH
        )
    loads = [
        pltpu.make_async_copy(src, dst, in_sem.at[k])
        for k, (src, dst) in enumerate(
            [
                (frequency_hbm, frequency_ref),
                (barrier_hbm, barrier_ref),
                (reactants_hbm, reactants_ref),
                (state_hbm, state_ref),
                (stoich_hbm, stoich_ref),
                (flags_hbm, flags_ref),
                (faces_hbm, faces_ref),
            ]
        )
    ]
    for load in loads:
        load.start()
    for load in loads:
        load.wait()

    rows[...] = jnp.zeros_like(rows)
    rows[:, 1536:] = jnp.where(
        lax.broadcasted_iota(jnp.int32, (8, 128), 0) >= 2, -1.0, 0.0
    )
    rows[0:1, :NR] = frequency_ref[...].reshape(1, NR)
    rows[1:2, :NR] = barrier_ref[...].reshape(1, NR)
    reactants = reactants_ref[...]
    lane = lax.broadcasted_iota(jnp.int32, (2, NR), 1)
    first = jnp.zeros((2, NR), jnp.int32)
    for g in range(1, GROUPS):
        first = jnp.where(lane >= g * GROUP_RATES, g * GROUP_STATE, first)
    local = reactants - first
    block = (local * 43) >> 8
    slot = (local - block * BS) * GROUP + block
    rows[2:4, :NR] = slot.astype(F32)
    rows[4:6, :NR] = reactants.astype(F32)
    columns[...] = jnp.transpose(rows[...])

    y_half[:, SPEC // 8 * 8 :, :] = jnp.zeros((2, STATE_ROWS - SPEC // 8 * 8, 128), F32)
    src_half[:, SPEC // 8 * 8 :, :] = jnp.zeros((2, STATE_ROWS - SPEC // 8 * 8, 128), F32)
    for h in range(2):
        y_half[h, :SPEC, :] = state_ref[:, h * 128 : (h + 1) * 128]
    s_hi[:, 1536:] = jnp.zeros((S_ROWS, 128), BF)
    s_lo[:, 1536:] = jnp.zeros((S_ROWS, 128), BF)
    s_hi[256:, :] = jnp.zeros((S_ROWS - 256, RATE_ROWS), BF)
    s_lo[256:, :] = jnp.zeros((S_ROWS - 256, RATE_ROWS), BF)
    for at in range(0, SPEC, 16):
        n = min(16, SPEC - at)
        hi, lo = split2(stoich_ref[at : at + n, :])
        s_hi[at : at + n, :NR] = hi
        s_lo[at : at + n, :NR] = lo

    for g in range(GROUPS):
        for start, n in chunks_of(g):
            spot = lax.rem(lax.broadcasted_iota(jnp.int32, (n, 3 * GROUP_STATE), 1), GROUP_STATE)
            for which in range(2):
                want = columns[start : start + n, 2 + which : 3 + which].astype(jnp.int32)
                hot = (want == spot).astype(F32).astype(BF)
                gather[which, start : start + n, :] = hot

    def spread(ref, g, h):
        return [ref[h, pl.ds(g * GROUP_STATE + m, GROUP, stride=BS), :] for m in range(BS)]

    def pieces(ref, g, h):
        at = g * GROUP_STATE
        lanes = slice(h * 128, (h + 1) * 128)
        return [ref[at + m * GROUP : at + (m + 1) * GROUP, lanes] for m in range(BS)]

    def put(ref, g, h, values):
        at = g * GROUP_STATE
        lanes = slice(h * 128, (h + 1) * 128)
        for m in range(BS):
            ref[at + m * GROUP : at + (m + 1) * GROUP, lanes] = values[m]

    def put_state(g, parts):
        for k, part in enumerate(split3(parts)):
            at = g * 3 * GROUP_STATE + k * GROUP_STATE
            y_split[at : at + GROUP_STATE, :] = part

    def reactant(which, g, start, n):
        at = g * 3 * GROUP_STATE
        return dot(gather[which, start : start + n, :], y_split[at : at + 3 * GROUP_STATE, :])

    r_hi[NR // 16 * 16 :, :] = jnp.zeros((RATE_ROWS - NR // 16 * 16, CELLS), BF)
    r_lo[NR // 16 * 16 :, :] = jnp.zeros((RATE_ROWS - NR // 16 * 16, CELLS), BF)
    fac[:, NR // 16 * 16 :, :] = jnp.zeros((2, RATE_ROWS - NR // 16 * 16, CELLS), BF)

    theta = 1.0 - 1.0 / state_ref[SPEC - 1 : SPEC, :]
    for g in range(GROUPS):
        for h in range(2):
            put(y0, g, h, spread(y_half, g, h))
        put_state(g, y0[g * GROUP_STATE : (g + 1) * GROUP_STATE, :])
        for start, n in chunks_of(g):
            k = columns[start : start + n, 0:1] * jnp.exp(columns[start : start + n, 1:2] * theta)
            coef[start : start + n, :] = k
            former = reactant(0, g, start, n)
            latter = reactant(1, g, start, n)
            by_first = k * latter
            fac[0, start : start + n, :] = by_first.astype(BF)
            fac[1, start : start + n, :] = (k * former).astype(BF)
            hi, lo = split2(by_first * former)
            r_hi[start : start + n, :] = hi
            r_lo[start : start + n, :] = lo

    def source_term():
        total = (
            dot(s_hi[...], r_hi[...]) + dot(s_lo[...], r_hi[...]) + dot(s_hi[...], r_lo[...])
        )
        for h in range(2):
            src_half[h, :S_ROWS, :] = total[:, h * 128 : (h + 1) * 128]

    def rates():
        for g in range(GROUPS):
            for start, n in chunks_of(g):
                k = coef[start : start + n, :]
                hi, lo = split2(k * reactant(0, g, start, n) * reactant(1, g, start, n))
                r_hi[start : start + n, :] = hi
                r_lo[start : start + n, :] = lo

    source_term()

    sub = lax.broadcasted_iota(jnp.int32, (GROUP, 1), 0) * BS
    for g in range(GROUPS):
        w, width = window_of(g)
        rows_here = min(GROUP_STATE, SPEC - g * GROUP_STATE)
        if rows_here < GROUP_STATE:
            s_tile[...] = jnp.zeros_like(s_tile)
        for t in range(0, width, 128):
            last = min(128, NR - w - t)
            if last > 0:
                s_tile[t // 128, :rows_here, :last] = stoich_ref[
                    g * GROUP_STATE : g * GROUP_STATE + rows_here, w + t : w + t + last
                ]
        slabs = [
            [s_tile[t, pl.ds(i, GROUP, stride=BS), :] for t in range(width // 128)]
            for i in range(BS)
        ]
        for which in range(2):
            reacts = rows[4 + which : 5 + which, w : w + width].astype(jnp.int32)
            masks = [reacts == sub + (g * GROUP_STATE + m) for m in range(BS)]
            for i in range(BS):
                s = jnp.concatenate(slabs[i], axis=1)
                for m in range(0, BS, 2):
                    pair = jnp.concatenate(
                        [jnp.where(masks[m], s, 0.0), jnp.where(masks[m + 1], s, 0.0)], axis=0
                    )
                    to = (i * BS + m) * GROUP
                    coupling[to : to + 16, which * width : (which + 1) * width] = pair.astype(BF)
        jacobian = dot(coupling[:, :width], fac[0, w : w + width, :]) + dot(
            coupling[:, width : 2 * width], fac[1, w : w + width, :]
        )
        lu[g, :, :] = jacobian

    def put_split(g, h, values):
        lanes = slice(h * 128, (h + 1) * 128)
        at = g * 3 * GROUP_STATE
        for m in range(0, BS, 2):
            both = jnp.concatenate([values[m], values[m + 1]], axis=0)
            for k, part in enumerate(split3(both)):
                to = at + k * GROUP_STATE + m * GROUP
                y_split[to : to + 16, lanes] = part

    def factors(g, h):
        lanes = slice(h * 128, (h + 1) * 128)
        return [
            [
                lu[g, (i * BS + m) * GROUP : (i * BS + m + 1) * GROUP, lanes]
                for m in range(BS)
            ]
            for i in range(BS)
        ]

    for g in range(GROUPS):
        for h in range(2):
            lanes = slice(h * 128, (h + 1) * 128)
            e = factors(g, h)
            e = [
                [(1.0 if i == m else 0.0) - SCALED * e[i][m] for m in range(BS)]
                for i in range(BS)
            ]
            e = factor(e)
            for i in range(BS):
                for m in range(BS):
                    lu[g, (i * BS + m) * GROUP : (i * BS + m + 1) * GROUP, lanes] = e[i][m]
            x = solve(e, [SCALED * s for s in spread(src_half, g, h)])
            put(u1, g, h, x)
            put_split(g, h, [y + A[0] * u for y, u in zip(pieces(y0, g, h), x)])
            y = pieces(y0, g, h)
            s = spread(src_half, g, h)
            put(explicit, g, h, [a + TIME_STEP * b for a, b in zip(y, s)])

    rates()
    source_term()
    for g in range(GROUPS):
        for h in range(2):
            e = factors(g, h)
            one = pieces(u1, g, h)
            x = solve(
                e, [SCALED * s + (GAMMA * C[0]) * u for s, u in zip(spread(src_half, g, h), one)]
            )
            put(u2, g, h, x)
            put_split(
                g,
                h,
                [y + A[1] * a + A[2] * b for y, a, b in zip(pieces(y0, g, h), one, x)],
            )

    rates()
    source_term()
    hot = jnp.concatenate(
        [
            lax.broadcasted_iota(jnp.int32, (CELLS, FACES), 0) == faces_ref[0:1, :],
            lax.broadcasted_iota(jnp.int32, (CELLS, FACES), 0) == faces_ref[1:2, :],
        ],
        axis=1,
    )
    hot = hot.astype(F32).astype(BF)
    for g in range(GROUPS):
        for h in range(2):
            lanes = slice(h * 128, (h + 1) * 128)
            e = factors(g, h)
            one = pieces(u1, g, h)
            two = pieces(u2, g, h)
            base = [SCALED * s for s in spread(src_half, g, h)]
            three = solve(
                e,
                [
                    s + (GAMMA * C[1]) * a + (GAMMA * C[2]) * b
                    for s, a, b in zip(base, one, two)
                ],
            )
            four = solve(
                e,
                [
                    s + (GAMMA * C[3]) * a + (GAMMA * C[4]) * b + (GAMMA * C[5]) * c
                    for s, a, b, c in zip(base, one, two, three)
                ],
            )
            stiff = flags_ref[lanes].reshape(1, 128) == 1
            out = [
                jnp.where(stiff, y + M[0] * a + M[1] * b + M[2] * c + M[3] * d, x)
                for y, a, b, c, d, x in zip(
                    pieces(y0, g, h), one, two, three, four, pieces(explicit, g, h)
                )
            ]
            for m in range(BS):
                y_half[h, pl.ds(g * GROUP_STATE + m, GROUP, stride=BS), :] = out[m]
        valid = min(GROUP_STATE, SPEC - g * GROUP_STATE)
        here = slice(g * GROUP_STATE, g * GROUP_STATE + GROUP_STATE)
        real = slice(g * GROUP_STATE, g * GROUP_STATE + valid)
        done = jnp.concatenate([y_half[0, here, :], y_half[1, here, :]], axis=1)
        advanced_ref[real, :] = done[:valid]
        at_faces = sum(dot(part, hot) for part in split3(done))
        for r in range(2):
            face[r, here, :] = at_faces[:, r * FACES : (r + 1) * FACES]

    pl.semaphore_wait(barrier, 2)
    sends = [
        pltpu.make_async_remote_copy(
            src_ref=face.at[1 - r],
            dst_ref=received.at[r],
            send_sem=send_sem.at[r],
            recv_sem=recv_sem.at[r],
            device_id={"dev": other},
            device_id_type=pl.DeviceIdType.MESH,
        )
        for r, other in ((0, up), (1, down))
    ]
    for send in sends:
        send.start()
    for r, (send, edge) in enumerate(zip(sends, (0, count - 1))):
        send.wait()
        inside = jnp.where(me == edge, 0.0, 1.0)
        jump_ref[:, r, :] = jnp.where(inside > 0.5, received[r, :SPEC, :], 0.0) - face[r, :SPEC, :]


def compute(state, flags, reactants, frequency, barrier, stoich, faces):
    return pl.pallas_call(
        kernel,
        out_shape=(
            jax.ShapeDtypeStruct((SPEC, CELLS), F32),
            jax.ShapeDtypeStruct((SPEC, 2, FACES), F32),
        ),
        in_specs=[pl.BlockSpec(memory_space=pltpu.HBM)] * 7,
        out_specs=[pl.BlockSpec(memory_space=pltpu.VMEM)] * 2,
        scratch_shapes=[
            pltpu.VMEM((SPEC, CELLS), F32),
            pltpu.VMEM((CELLS,), jnp.int32),
            pltpu.VMEM((2, NR), jnp.int32),
            pltpu.VMEM((NR,), F32),
            pltpu.VMEM((NR,), F32),
            pltpu.VMEM((SPEC, NR), F32),
            pltpu.VMEM((2, FACES), jnp.int32),
            pltpu.SemaphoreType.DMA((7,)),
            pltpu.VMEM((2, STATE_ROWS, FACES), F32),
            pltpu.VMEM((2, STATE_ROWS, FACES), F32),
            pltpu.SemaphoreType.DMA((2,)),
            pltpu.SemaphoreType.DMA((2,)),
            pltpu.VMEM((8, RATE_ROWS), F32),
            pltpu.VMEM((RATE_ROWS, 8), F32),
            pltpu.VMEM((S_ROWS, RATE_ROWS), BF),
            pltpu.VMEM((S_ROWS, RATE_ROWS), BF),
            pltpu.VMEM((3, GROUP_STATE, 128), F32),
            pltpu.VMEM((2, STATE_ROWS, 128), F32),
            pltpu.VMEM((2, STATE_ROWS, 128), F32),
            pltpu.VMEM((STATE_ROWS, CELLS), F32),
            pltpu.VMEM((2, RATE_ROWS, 3 * GROUP_STATE), BF),
            pltpu.VMEM((3 * STATE_ROWS, CELLS), BF),
            pltpu.VMEM((RATE_ROWS, CELLS), F32),
            pltpu.VMEM((RATE_ROWS, CELLS), BF),
            pltpu.VMEM((RATE_ROWS, CELLS), BF),
            pltpu.VMEM((2, RATE_ROWS, CELLS), BF),
            pltpu.VMEM((STATE_ROWS, 768), BF),
            pltpu.VMEM((GROUPS, STATE_ROWS, CELLS), F32),
            pltpu.VMEM((STATE_ROWS, CELLS), F32),
            pltpu.VMEM((STATE_ROWS, CELLS), F32),
            pltpu.VMEM((STATE_ROWS, CELLS), F32),
        ],
        compiler_params=pltpu.CompilerParams(vmem_limit_bytes=60 * 1024 * 1024, collective_id=0, has_side_effects=True),
        cost_estimate=pl.CostEstimate(
            flops=4_000_000_000, bytes_accessed=3_000_000, transcendentals=400_000
        ),
    )(
        state,
        flags,
        reactants,
        frequency,
        barrier,
        stoich,
        faces,
    )


def on_device(state, flags, reactants, frequency, barrier, stoich, faces):
    return compute(state, flags, reactants, frequency, barrier, stoich, faces)


def solution(mesh):
    cells = P(None, ("grp", "dev"))
    return jax.shard_map(
        on_device,
        mesh=mesh,
        in_specs=(cells, P(("grp", "dev")), P(), P(), P(), P(), cells),
        out_specs=(cells, P(None, None, ("grp", "dev"))),
        check_vma=False,
    )
```

```python
import jax
import jax.numpy as jnp
from jax import lax
from jax.experimental import pallas as pl
from jax.experimental.pallas import tpu as pltpu
from jax.sharding import PartitionSpec as P

NB = 43
BS = 6
RPB = 36
SPEC = 258
NR = 1548
CELLS = 256
FACES = 128

GROUP = 8
GROUPS = 6
GROUP_STATE = GROUP * BS
GROUP_RATES = GROUP * RPB
STATE_ROWS = GROUPS * GROUP_STATE
LAST_RATES = 112
RATE_ROWS = 1664
CHUNK = 96
S_ROWS = 272

TIME_STEP = 0.01
GAMMA = 0.5
SCALED = TIME_STEP * GAMMA
A = (2.0, 1.867943637803922, 0.2344449711399156)
C = (
    -7.13761503641231,
    2.580708087951457,
    0.6515950076447975,
    -2.137148994382534,
    -0.3214669691237626,
    -0.6949742501781779,
)
M = (2.255570073418735, 0.2870493262186792, 0.435317943184018, 1.093502252409163)

BF = jnp.bfloat16
F32 = jnp.float32


def dot(a, b):
    return jnp.dot(a, b, preferred_element_type=F32)


def split2(x):
    hi = x.astype(BF)
    return hi, (x - hi.astype(F32)).astype(BF)


def split3(x):
    hi = x.astype(BF)
    rest = x - hi.astype(F32)
    mid = rest.astype(BF)
    return hi, mid, (rest - mid.astype(F32)).astype(BF)


def chunks_of(group):
    start = group * GROUP_RATES
    if group == GROUPS - 1:
        return [(start, LAST_RATES)]
    return [(start + k, CHUNK) for k in range(0, GROUP_RATES, CHUNK)]


def window_of(group):
    start = group * GROUP_RATES // 128 * 128
    return start, (256 if group == GROUPS - 1 else 384)


def factor(e):
    for p in range(BS):
        inverse = 1.0 / e[p][p]
        e[p][p] = inverse
        for t in range(p + 1, BS):
            e[t][p] = e[t][p] * inverse
            for c in range(p + 1, BS):
                e[t][c] = e[t][c] - e[t][p] * e[p][c]
    return e


def solve(e, b):
    x = list(b)
    for t in range(BS):
        for c in range(t):
            x[t] = x[t] - e[t][c] * x[c]
    for t in reversed(range(BS)):
        for c in range(t + 1, BS):
            x[t] = x[t] - e[t][c] * x[c]
        x[t] = x[t] * e[t][t]
    return x


def kernel(
    state_hbm,
    flags_hbm,
    reactants_hbm,
    frequency_hbm,
    barrier_hbm,
    stoich_hbm,
    faces_hbm,
    advanced_ref,
    jump_ref,
    state_ref,
    flags_ref,
    reactants_ref,
    frequency_ref,
    barrier_ref,
    stoich_ref,
    faces_ref,
    in_sem,
    face,
    received,
    send_sem,
    recv_sem,
    rows,
    columns,
    s_hi,
    s_lo,
    s_tile,
    y_half,
    src_half,
    y0,
    gather,
    y_split,
    coef,
    r_hi,
    r_lo,
    fac,
    coupling,
    lu,
    explicit,
    u1,
    u2,
):
    me = lax.axis_index("dev")
    count = lax.axis_size("dev")
    up = lax.rem(me + 1, count)
    down = lax.rem(me + count - 1, count)
    has_up = me < count - 1
    has_down = me > 0
    barrier = pltpu.get_barrier_semaphore()

    def greet(other):
        pl.semaphore_signal(
            barrier, inc=1, device_id={"dev": other}, device_id_type=pl.DeviceIdType.MESH
        )

    @pl.when(has_up)
    def _():
        greet(up)

    @pl.when(has_down)
    def _():
        greet(down)

    loads = [
        pltpu.make_async_copy(src, dst, in_sem.at[k])
        for k, (src, dst) in enumerate(
            [
                (frequency_hbm, frequency_ref),
                (barrier_hbm, barrier_ref),
                (reactants_hbm, reactants_ref),
                (state_hbm, state_ref),
                (stoich_hbm, stoich_ref),
                (flags_hbm, flags_ref),
                (faces_hbm, faces_ref),
            ]
        )
    ]
    for load in loads:
        load.start()
    for load in loads:
        load.wait()

    rows[...] = jnp.zeros_like(rows)
    rows[:, 1536:] = jnp.where(
        lax.broadcasted_iota(jnp.int32, (8, 128), 0) >= 2, -1.0, 0.0
    )
    rows[0:1, :NR] = frequency_ref[...].reshape(1, NR)
    rows[1:2, :NR] = barrier_ref[...].reshape(1, NR)
    reactants = reactants_ref[...]
    lane = lax.broadcasted_iota(jnp.int32, (2, NR), 1)
    first = jnp.zeros((2, NR), jnp.int32)
    for g in range(1, GROUPS):
        first = jnp.where(lane >= g * GROUP_RATES, g * GROUP_STATE, first)
    local = reactants - first
    block = (local * 43) >> 8
    slot = (local - block * BS) * GROUP + block
    rows[2:4, :NR] = slot.astype(F32)
    rows[4:6, :NR] = reactants.astype(F32)
    columns[...] = jnp.transpose(rows[...])

    y_half[:, SPEC // 8 * 8 :, :] = jnp.zeros((2, STATE_ROWS - SPEC // 8 * 8, 128), F32)
    src_half[:, SPEC // 8 * 8 :, :] = jnp.zeros((2, STATE_ROWS - SPEC // 8 * 8, 128), F32)
    for h in range(2):
        y_half[h, :SPEC, :] = state_ref[:, h * 128 : (h + 1) * 128]
    s_hi[:, 1536:] = jnp.zeros((S_ROWS, 128), BF)
    s_lo[:, 1536:] = jnp.zeros((S_ROWS, 128), BF)
    s_hi[256:, :] = jnp.zeros((S_ROWS - 256, RATE_ROWS), BF)
    s_lo[256:, :] = jnp.zeros((S_ROWS - 256, RATE_ROWS), BF)
    for at in range(0, SPEC, 16):
        n = min(16, SPEC - at)
        hi, lo = split2(stoich_ref[at : at + n, :])
        s_hi[at : at + n, :NR] = hi
        s_lo[at : at + n, :NR] = lo

    for g in range(GROUPS):
        for start, n in chunks_of(g):
            spot = lax.rem(lax.broadcasted_iota(jnp.int32, (n, 3 * GROUP_STATE), 1), GROUP_STATE)
            for which in range(2):
                want = columns[start : start + n, 2 + which : 3 + which].astype(jnp.int32)
                hot = (want == spot).astype(F32).astype(BF)
                gather[which, start : start + n, :] = hot

    def spread(ref, g, h):
        return [ref[h, pl.ds(g * GROUP_STATE + m, GROUP, stride=BS), :] for m in range(BS)]

    def pieces(ref, g, h):
        at = g * GROUP_STATE
        lanes = slice(h * 128, (h + 1) * 128)
        return [ref[at + m * GROUP : at + (m + 1) * GROUP, lanes] for m in range(BS)]

    def put(ref, g, h, values):
        at = g * GROUP_STATE
        lanes = slice(h * 128, (h + 1) * 128)
        for m in range(BS):
            ref[at + m * GROUP : at + (m + 1) * GROUP, lanes] = values[m]

    def put_state(g, parts):
        for k, part in enumerate(split3(parts)):
            at = g * 3 * GROUP_STATE + k * GROUP_STATE
            y_split[at : at + GROUP_STATE, :] = part

    def reactant(which, g, start, n):
        at = g * 3 * GROUP_STATE
        return dot(gather[which, start : start + n, :], y_split[at : at + 3 * GROUP_STATE, :])

    r_hi[NR // 16 * 16 :, :] = jnp.zeros((RATE_ROWS - NR // 16 * 16, CELLS), BF)
    r_lo[NR // 16 * 16 :, :] = jnp.zeros((RATE_ROWS - NR // 16 * 16, CELLS), BF)
    fac[:, NR // 16 * 16 :, :] = jnp.zeros((2, RATE_ROWS - NR // 16 * 16, CELLS), BF)

    theta = 1.0 - 1.0 / state_ref[SPEC - 1 : SPEC, :]
    for g in range(GROUPS):
        for h in range(2):
            put(y0, g, h, spread(y_half, g, h))
        put_state(g, y0[g * GROUP_STATE : (g + 1) * GROUP_STATE, :])
        for start, n in chunks_of(g):
            k = columns[start : start + n, 0:1] * jnp.exp(columns[start : start + n, 1:2] * theta)
            coef[start : start + n, :] = k
            former = reactant(0, g, start, n)
            latter = reactant(1, g, start, n)
            by_first = k * latter
            fac[0, start : start + n, :] = by_first.astype(BF)
            fac[1, start : start + n, :] = (k * former).astype(BF)
            hi, lo = split2(by_first * former)
            r_hi[start : start + n, :] = hi
            r_lo[start : start + n, :] = lo

    def source_term():
        total = (
            dot(s_hi[...], r_hi[...]) + dot(s_lo[...], r_hi[...]) + dot(s_hi[...], r_lo[...])
        )
        for h in range(2):
            src_half[h, :S_ROWS, :] = total[:, h * 128 : (h + 1) * 128]

    def rates():
        for g in range(GROUPS):
            for start, n in chunks_of(g):
                k = coef[start : start + n, :]
                hi, lo = split2(k * reactant(0, g, start, n) * reactant(1, g, start, n))
                r_hi[start : start + n, :] = hi
                r_lo[start : start + n, :] = lo

    source_term()

    sub = lax.broadcasted_iota(jnp.int32, (GROUP, 1), 0) * BS
    for g in range(GROUPS):
        w, width = window_of(g)
        rows_here = min(GROUP_STATE, SPEC - g * GROUP_STATE)
        if rows_here < GROUP_STATE:
            s_tile[...] = jnp.zeros_like(s_tile)
        for t in range(0, width, 128):
            last = min(128, NR - w - t)
            if last > 0:
                s_tile[t // 128, :rows_here, :last] = stoich_ref[
                    g * GROUP_STATE : g * GROUP_STATE + rows_here, w + t : w + t + last
                ]
        slabs = [
            [s_tile[t, pl.ds(i, GROUP, stride=BS), :] for t in range(width // 128)]
            for i in range(BS)
        ]
        for which in range(2):
            reacts = rows[4 + which : 5 + which, w : w + width].astype(jnp.int32)
            masks = [reacts == sub + (g * GROUP_STATE + m) for m in range(BS)]
            for i in range(BS):
                s = jnp.concatenate(slabs[i], axis=1)
                for m in range(0, BS, 2):
                    pair = jnp.concatenate(
                        [jnp.where(masks[m], s, 0.0), jnp.where(masks[m + 1], s, 0.0)], axis=0
                    )
                    to = (i * BS + m) * GROUP
                    coupling[to : to + 16, which * width : (which + 1) * width] = pair.astype(BF)
        jacobian = dot(coupling[:, :width], fac[0, w : w + width, :]) + dot(
            coupling[:, width : 2 * width], fac[1, w : w + width, :]
        )
        lu[g, :, :] = jacobian

    def put_split(g, h, values):
        lanes = slice(h * 128, (h + 1) * 128)
        at = g * 3 * GROUP_STATE
        for m in range(0, BS, 2):
            both = jnp.concatenate([values[m], values[m + 1]], axis=0)
            for k, part in enumerate(split3(both)):
                to = at + k * GROUP_STATE + m * GROUP
                y_split[to : to + 16, lanes] = part

    def factors(g, h):
        lanes = slice(h * 128, (h + 1) * 128)
        return [
            [
                lu[g, (i * BS + m) * GROUP : (i * BS + m + 1) * GROUP, lanes]
                for m in range(BS)
            ]
            for i in range(BS)
        ]

    for g in range(GROUPS):
        for h in range(2):
            lanes = slice(h * 128, (h + 1) * 128)
            e = factors(g, h)
            e = [
                [(1.0 if i == m else 0.0) - SCALED * e[i][m] for m in range(BS)]
                for i in range(BS)
            ]
            e = factor(e)
            for i in range(BS):
                for m in range(BS):
                    lu[g, (i * BS + m) * GROUP : (i * BS + m + 1) * GROUP, lanes] = e[i][m]
            x = solve(e, [SCALED * s for s in spread(src_half, g, h)])
            put(u1, g, h, x)
            put_split(g, h, [y + A[0] * u for y, u in zip(pieces(y0, g, h), x)])
            y = pieces(y0, g, h)
            s = spread(src_half, g, h)
            put(explicit, g, h, [a + TIME_STEP * b for a, b in zip(y, s)])

    rates()
    source_term()
    for g in range(GROUPS):
        for h in range(2):
            e = factors(g, h)
            one = pieces(u1, g, h)
            x = solve(
                e, [SCALED * s + (GAMMA * C[0]) * u for s, u in zip(spread(src_half, g, h), one)]
            )
            put(u2, g, h, x)
            put_split(
                g,
                h,
                [y + A[1] * a + A[2] * b for y, a, b in zip(pieces(y0, g, h), one, x)],
            )

    rates()
    source_term()
    hot = jnp.concatenate(
        [
            lax.broadcasted_iota(jnp.int32, (CELLS, FACES), 0) == faces_ref[0:1, :],
            lax.broadcasted_iota(jnp.int32, (CELLS, FACES), 0) == faces_ref[1:2, :],
        ],
        axis=1,
    )
    hot = hot.astype(F32).astype(BF)
    for g in range(GROUPS):
        for h in range(2):
            lanes = slice(h * 128, (h + 1) * 128)
            e = factors(g, h)
            one = pieces(u1, g, h)
            two = pieces(u2, g, h)
            base = [SCALED * s for s in spread(src_half, g, h)]
            three = solve(
                e,
                [
                    s + (GAMMA * C[1]) * a + (GAMMA * C[2]) * b
                    for s, a, b in zip(base, one, two)
                ],
            )
            four = solve(
                e,
                [
                    s + (GAMMA * C[3]) * a + (GAMMA * C[4]) * b + (GAMMA * C[5]) * c
                    for s, a, b, c in zip(base, one, two, three)
                ],
            )
            stiff = flags_ref[lanes].reshape(1, 128) == 1
            out = [
                jnp.where(stiff, y + M[0] * a + M[1] * b + M[2] * c + M[3] * d, x)
                for y, a, b, c, d, x in zip(
                    pieces(y0, g, h), one, two, three, four, pieces(explicit, g, h)
                )
            ]
            for m in range(BS):
                y_half[h, pl.ds(g * GROUP_STATE + m, GROUP, stride=BS), :] = out[m]
        valid = min(GROUP_STATE, SPEC - g * GROUP_STATE)
        here = slice(g * GROUP_STATE, g * GROUP_STATE + GROUP_STATE)
        real = slice(g * GROUP_STATE, g * GROUP_STATE + valid)
        done = jnp.concatenate([y_half[0, here, :], y_half[1, here, :]], axis=1)
        advanced_ref[real, :] = done[:valid]
        at_faces = sum(dot(part, hot) for part in split3(done))
        for r in range(2):
            face[r, here, :] = at_faces[:, r * FACES : (r + 1) * FACES]

    def neighbour(r, other):
        return pltpu.make_async_remote_copy(
            src_ref=face.at[r],
            dst_ref=received.at[1 - r],
            send_sem=send_sem.at[r],
            recv_sem=recv_sem.at[1 - r],
            device_id={"dev": other},
            device_id_type=pl.DeviceIdType.MESH,
        )

    pl.semaphore_wait(barrier, has_up.astype(jnp.int32) + has_down.astype(jnp.int32))

    @pl.when(has_down)
    def _():
        neighbour(0, down).start()

    @pl.when(has_up)
    def _():
        neighbour(1, up).start()

    for r, there, other in ((0, has_down, down), (1, has_up, up)):

        @pl.when(there)
        def _(r=r, other=other):
            neighbour(1 - r, other).wait_recv()
            jump_ref[:, r, :] = received[r, :SPEC, :] - face[r, :SPEC, :]
            neighbour(r, other).wait_send()

        @pl.when(jnp.logical_not(there))
        def _(r=r):
            jump_ref[:, r, :] = 0.0 - face[r, :SPEC, :]


def compute(state, flags, reactants, frequency, barrier, stoich, faces):
    return pl.pallas_call(
        kernel,
        out_shape=(
            jax.ShapeDtypeStruct((SPEC, CELLS), F32),
            jax.ShapeDtypeStruct((SPEC, 2, FACES), F32),
        ),
        in_specs=[pl.BlockSpec(memory_space=pltpu.HBM)] * 7,
        out_specs=[pl.BlockSpec(memory_space=pltpu.VMEM)] * 2,
        scratch_shapes=[
            pltpu.VMEM((SPEC, CELLS), F32),
            pltpu.VMEM((CELLS,), jnp.int32),
            pltpu.VMEM((2, NR), jnp.int32),
            pltpu.VMEM((NR,), F32),
            pltpu.VMEM((NR,), F32),
            pltpu.VMEM((SPEC, NR), F32),
            pltpu.VMEM((2, FACES), jnp.int32),
            pltpu.SemaphoreType.DMA((7,)),
            pltpu.VMEM((2, STATE_ROWS, FACES), F32),
            pltpu.VMEM((2, STATE_ROWS, FACES), F32),
            pltpu.SemaphoreType.DMA((2,)),
            pltpu.SemaphoreType.DMA((2,)),
            pltpu.VMEM((8, RATE_ROWS), F32),
            pltpu.VMEM((RATE_ROWS, 8), F32),
            pltpu.VMEM((S_ROWS, RATE_ROWS), BF),
            pltpu.VMEM((S_ROWS, RATE_ROWS), BF),
            pltpu.VMEM((3, GROUP_STATE, 128), F32),
            pltpu.VMEM((2, STATE_ROWS, 128), F32),
            pltpu.VMEM((2, STATE_ROWS, 128), F32),
            pltpu.VMEM((STATE_ROWS, CELLS), F32),
            pltpu.VMEM((2, RATE_ROWS, 3 * GROUP_STATE), BF),
            pltpu.VMEM((3 * STATE_ROWS, CELLS), BF),
            pltpu.VMEM((RATE_ROWS, CELLS), F32),
            pltpu.VMEM((RATE_ROWS, CELLS), BF),
            pltpu.VMEM((RATE_ROWS, CELLS), BF),
            pltpu.VMEM((2, RATE_ROWS, CELLS), BF),
            pltpu.VMEM((STATE_ROWS, 768), BF),
            pltpu.VMEM((GROUPS, STATE_ROWS, CELLS), F32),
            pltpu.VMEM((STATE_ROWS, CELLS), F32),
            pltpu.VMEM((STATE_ROWS, CELLS), F32),
            pltpu.VMEM((STATE_ROWS, CELLS), F32),
        ],
        compiler_params=pltpu.CompilerParams(vmem_limit_bytes=32 * 1024 * 1024, collective_id=0, has_side_effects=True),
        cost_estimate=pl.CostEstimate(
            flops=4_000_000_000, bytes_accessed=3_000_000, transcendentals=400_000
        ),
    )(
        state,
        flags,
        reactants,
        frequency,
        barrier,
        stoich,
        faces,
    )


def on_device(state, flags, reactants, frequency, barrier, stoich, faces):
    args = [pltpu.with_memory_space_constraint(x, pltpu.HBM) for x in (state, flags, reactants, frequency, barrier, stoich, faces)]
    return compute(*args)


def solution(mesh):
    cells = P(None, ("grp", "dev"))
    return jax.shard_map(
        on_device,
        mesh=mesh,
        in_specs=(cells, P(("grp", "dev")), P(), P(), P(), P(), cells),
        out_specs=(cells, P(None, None, ("grp", "dev"))),
        check_vma=False,
    )
```

```python
import jax
import jax.numpy as jnp
from jax import lax
from jax.experimental import pallas as pl
from jax.experimental.pallas import tpu as pltpu
from jax.sharding import PartitionSpec as P

NB = 43
BS = 6
RPB = 36
SPEC = 258
NR = 1548
CELLS = 256
FACES = 128

TRIO = 3
TRIOS = 15
TRIO_STATE = TRIO * BS
TRIO_RATES = TRIO * RPB
TRIO_ROWS = 24
JAC_ROWS = BS * TRIO_ROWS
LONG = 8 * TRIO_STATE
STATE_ROWS = 2 * LONG + 8
RATE_ROWS = 1552
FAC_ROWS = 1664
S_ROWS = 272
MAIN = 1536
HALF = MAIN // 2

TIME_STEP = 0.01
GAMMA = 0.5
SCALED = TIME_STEP * GAMMA
A = (2.0, 1.867943637803922, 0.2344449711399156)
C = (
    -7.13761503641231,
    2.580708087951457,
    0.6515950076447975,
    -2.137148994382534,
    -0.3214669691237626,
    -0.6949742501781779,
)
M = (2.255570073418735, 0.2870493262186792, 0.435317943184018, 1.093502252409163)

BF = jnp.bfloat16
F32 = jnp.float32
I32 = jnp.int32
MESH = pl.DeviceIdType.MESH

ROW_GATHER = lax.GatherDimensionNumbers(
    offset_dims=(),
    collapsed_slice_dims=(0,),
    start_index_map=(0,),
    operand_batching_dims=(1,),
    start_indices_batching_dims=(1,),
)


def dot(a, b):
    return jnp.dot(a, b, preferred_element_type=F32)


def split2(x):
    hi = x.astype(BF)
    return hi, (x - hi.astype(F32)).astype(BF)


def split3(x):
    hi = x.astype(BF)
    rest = x - hi.astype(F32)
    mid = rest.astype(BF)
    return hi, mid, (rest - mid.astype(F32)).astype(BF)


def take_rows(x, index):
    return lax.gather(
        x,
        index[..., None],
        ROW_GATHER,
        slice_sizes=(1, 1),
        mode=lax.GatherScatterMode.PROMISE_IN_BOUNDS,
    )


def factor(e):
    for p in range(BS):
        inverse = 1.0 / e[p][p]
        e[p][p] = inverse
        for t in range(p + 1, BS):
            e[t][p] = e[t][p] * inverse
            for c in range(p + 1, BS):
                e[t][c] = e[t][c] - e[t][p] * e[p][c]
    return e


def solve(e, b):
    x = list(b)
    for t in range(BS):
        for c in range(t):
            x[t] = x[t] - e[t][c] * x[c]
    for t in reversed(range(BS)):
        for c in range(t + 1, BS):
            x[t] = x[t] - e[t][c] * x[c]
        x[t] = x[t] * e[t][t]
    return x


def both(a, b):
    return jnp.concatenate([a, b], axis=0)


def lanes(h):
    return slice(h * 128, (h + 1) * 128)


CHUNKS = [(r, s, h) for s in range(2) for h in range(2) for r in range(TRIO)]


def kernel(
    state_hbm,
    flags_hbm,
    reactants_hbm,
    frequency_hbm,
    barrier_hbm,
    stoich_hbm,
    faces_hbm,
    advanced_ref,
    jump_ref,
    state_ref,
    flags_ref,
    reactants_ref,
    frequency_ref,
    barrier_ref,
    stoich_ref,
    faces_ref,
    in_sem,
    face,
    received,
    send_sem,
    recv_sem,
    rows,
    columns,
    index,
    coef,
    y0,
    y,
    part,
    s_split,
    s_tail,
    tail,
    trio,
    r_hi,
    r_lo,
    fac,
    jac,
    lu,
    u1,
    u2,
    explicit,
):
    me = lax.axis_index("dev")
    count = lax.axis_size("dev")
    up = lax.rem(me + 1, count)
    down = lax.rem(me + count - 1, count)
    has_up = me < count - 1
    has_down = me > 0
    barrier = pltpu.get_barrier_semaphore()

    def greet(other):
        pl.semaphore_signal(barrier, inc=1, device_id={"dev": other}, device_id_type=MESH)

    @pl.when(has_up)
    def _():
        greet(up)

    @pl.when(has_down)
    def _():
        greet(down)

    loads = [
        pltpu.make_async_copy(src, dst, in_sem.at[k])
        for k, (src, dst) in enumerate(
            [
                (reactants_hbm, reactants_ref),
                (frequency_hbm, frequency_ref),
                (barrier_hbm, barrier_ref),
                (state_hbm, state_ref),
                (stoich_hbm, stoich_ref),
                (flags_hbm, flags_ref),
                (faces_hbm, faces_ref),
            ]
        )
    ]
    for load in loads:
        load.start()

    rows[...] = jnp.zeros_like(rows)
    tail[...] = jnp.zeros_like(tail)
    jac[:, TRIOS * JAC_ROWS :, :] = jnp.zeros((2, JAC_ROWS, 128), F32)
    y0[:, SPEC // 8 * 8 :, :] = jnp.zeros((2, STATE_ROWS - SPEC // 8 * 8, 128), F32)
    part[:, :, S_ROWS:, :] = jnp.zeros((2, 2, STATE_ROWS - S_ROWS, 128), F32)
    fac[:, RATE_ROWS:, :] = jnp.zeros((2, FAC_ROWS - RATE_ROWS, CELLS), BF)
    for load in loads:
        load.wait()

    reactants = reactants_ref[...]
    first = ((lax.broadcasted_iota(I32, (2, NR), 1) * 1821) >> 16) * BS
    rows[0:1, :NR] = frequency_ref[...].reshape(1, NR)
    rows[1:2, :NR] = barrier_ref[...].reshape(1, NR)
    rows[2:4, :NR] = (reactants - first).astype(F32)
    rows[4:6, :NR] = reactants.astype(F32)
    columns[...] = jnp.transpose(rows[...])

    for h in range(2):
        y0[h, :SPEC, :] = state_ref[:, lanes(h)]

    sub = lax.broadcasted_iota(I32, (8, 128), 0)

    def reactant(ref, h, at, want):
        one = at // RPB
        two = min((at + 7) // RPB, NB - 1)
        got = take_rows(ref[h, one * BS : one * BS + 8, :], want)
        if two != one:
            other = take_rows(ref[h, two * BS : two * BS + 8, :], want)
            got = jnp.where(sub < two * RPB - at, got, other)
        return got

    def put_rates(at, h, values):
        hi, lo = split2(both(*values))
        r_hi[at : at + 16, lanes(h)] = hi
        r_lo[at : at + 16, lanes(h)] = lo

    theta = 1.0 - 1.0 / state_ref[SPEC - 1 : SPEC, :]
    for at in range(0, RATE_ROWS, 16):
        wants, freq, ener = [], [], []
        for k in (at, at + 8):
            freq.append(jnp.broadcast_to(columns[k : k + 8, 0:1], (8, 128)))
            ener.append(jnp.broadcast_to(columns[k : k + 8, 1:2], (8, 128)))
            want = [
                jnp.broadcast_to(columns[k : k + 8, 2 + w : 3 + w], (8, 128)).astype(I32)
                for w in range(2)
            ]
            for w in range(2):
                index[w, k : k + 8, :] = want[w]
            wants.append(want)
        for h in range(2):
            one, two, rate = [], [], []
            for q, k in enumerate((at, at + 8)):
                c = freq[q] * jnp.exp(ener[q] * theta[:, lanes(h)])
                coef[h, k : k + 8, :] = c
                former = reactant(y0, h, k, wants[q][0])
                latter = reactant(y0, h, k, wants[q][1])
                one.append(c * latter)
                two.append(c * former)
                rate.append(one[-1] * former)
            fac[0, at : at + 16, lanes(h)] = both(*one).astype(BF)
            fac[1, at : at + 16, lanes(h)] = both(*two).astype(BF)
            put_rates(at, h, rate)

    for at in range(0, SPEC, 16):
        n = min(16, SPEC - at)
        x = stoich_ref[at : at + n, :MAIN]
        if n < 16:
            x = both(x, jnp.zeros((16 - n, MAIN), F32))
        hi, lo = split2(x)
        s_split[at : at + 16, :] = hi
        s_split[S_ROWS + at : S_ROWS + at + 16, :] = lo
    tail[:SPEC, : NR - MAIN] = stoich_ref[:, MAIN:]
    for at in range(0, S_ROWS, 16):
        x = tail[at : at + 16, :]
        hi = x.astype(BF).astype(F32)
        lo = x - hi
        s_tail[at : at + 16, :] = (hi + pltpu.roll(lo, 16, 1) + pltpu.roll(hi, 32, 1)).astype(BF)

    def source_term():
        for k in range(2):
            span = slice(k * HALF, (k + 1) * HALF)
            long = dot(s_split[:, span], r_hi[span, :])
            total = long[:S_ROWS] + long[S_ROWS:] + dot(s_split[:S_ROWS, span], r_lo[span, :])
            if k == 1:
                last = jnp.concatenate([r_hi[MAIN:, :], r_hi[MAIN:, :], r_lo[MAIN:, :]], axis=0)
                total = total + dot(s_tail[:, :48], last)
            for h in range(2):
                part[k, h, :S_ROWS, :] = total[:, lanes(h)]

    def rates():
        for at in range(0, RATE_ROWS, 16):
            wants = [[index[w, k : k + 8, :] for w in range(2)] for k in (at, at + 8)]
            for h in range(2):
                put_rates(
                    at,
                    h,
                    [
                        coef[h, k : k + 8, :]
                        * reactant(y, h, k, want[0])
                        * reactant(y, h, k, want[1])
                        for k, want in zip((at, at + 8), wants)
                    ],
                )

    source_term()

    shift = ((lax.broadcasted_iota(I32, (TRIO_ROWS, 1), 0) * 43) >> 8) * BS
    for t in range(TRIOS):
        start = t * TRIO_RATES // 16 * 16
        low = start // 128 * 128
        top = t * TRIO_STATE
        n = min(TRIO_STATE, SPEC - top)
        wide = min(256, NR - low)
        if wide < 256 or n < TRIO_STATE:
            trio[...] = jnp.zeros_like(trio)
        trio[:n, :wide] = stoich_ref[top : top + n, low : low + wide] * -SCALED
        x = trio[...]
        reacts = rows[:, low : low + 256]
        if start > low:
            x = pltpu.roll(x, 256 - (start - low), 1)
            reacts = pltpu.roll(reacts, 256 - (start - low), 1)
        x = x[:, :128]
        reacts = reacts[:, :128]
        sides = []
        for w in range(2):
            where = reacts[4 + w : 5 + w, :].astype(I32) - (shift + top)
            sides.append(
                jnp.concatenate([jnp.where(where == m, x, 0.0) for m in range(BS)], axis=0)
            )
        coupling = jnp.concatenate([side.astype(BF) for side in sides], axis=1)
        factors_here = both(fac[0, start : start + 128, :], fac[1, start : start + 128, :])
        block = dot(coupling, factors_here)
        for h in range(2):
            jac[h, t * JAC_ROWS : (t + 1) * JAC_ROWS, :] = block[:, lanes(h)]

    def state_rows(r, s, m):
        return pl.ds(s * LONG + r * BS + m, 8, stride=TRIO_STATE)

    def spread(ref, r, s, h):
        return [ref[h, state_rows(r, s, m), :] for m in range(BS)]

    def source(r, s, h):
        return [
            part[0, h, state_rows(r, s, m), :] + part[1, h, state_rows(r, s, m), :]
            for m in range(BS)
        ]

    def put_state(ref, r, s, h, values):
        for m in range(BS):
            ref[h, state_rows(r, s, m), :] = values[m]

    def keep(ref, k, values):
        for m in range(BS):
            ref[k, m] = values[m]

    def kept(ref, k):
        return [ref[k, m] for m in range(BS)]

    def factors(k):
        return [[lu[k, i, m] for m in range(BS)] for i in range(BS)]

    for k, (r, s, h) in enumerate(CHUNKS):
        e = [
            [
                jac[h, pl.ds(s * 8 * JAC_ROWS + m * TRIO_ROWS + r * BS + i, 8, stride=JAC_ROWS), :]
                for m in range(BS)
            ]
            for i in range(BS)
        ]
        for i in range(BS):
            e[i][i] = 1.0 + e[i][i]
        e = factor(e)
        for i in range(BS):
            for m in range(BS):
                lu[k, i, m] = e[i][m]
        rhs = source(r, s, h)
        x = solve(e, rhs)
        start = spread(y0, r, s, h)
        keep(u1, k, x)
        keep(explicit, k, [a + TIME_STEP * b for a, b in zip(start, rhs)])
        put_state(y, r, s, h, [a + (SCALED * A[0]) * b for a, b in zip(start, x)])

    rates()
    source_term()
    for k, (r, s, h) in enumerate(CHUNKS):
        one = kept(u1, k)
        x = solve(factors(k), [a + (GAMMA * C[0]) * b for a, b in zip(source(r, s, h), one)])
        keep(u2, k, x)
        put_state(
            y,
            r,
            s,
            h,
            [
                a + (SCALED * A[1]) * b + (SCALED * A[2]) * c
                for a, b, c in zip(spread(y0, r, s, h), one, x)
            ],
        )

    rates()
    source_term()

    spot = lax.broadcasted_iota(I32, (CELLS, FACES), 0)
    hot = jnp.concatenate([spot == faces_ref[0:1, :], spot == faces_ref[1:2, :]], axis=1)
    hot = hot.astype(F32).astype(BF)

    def neighbour(r, s, other):
        here = pl.ds(s * LONG, LONG)
        return pltpu.make_async_remote_copy(
            src_ref=face.at[r, here],
            dst_ref=received.at[1 - r, here],
            send_sem=send_sem.at[r, s],
            recv_sem=recv_sem.at[1 - r, s],
            device_id={"dev": other},
            device_id_type=MESH,
        )

    for s in range(2):
        for k, (r, s_k, h) in enumerate(CHUNKS):
            if s_k != s:
                continue
            e = factors(k)
            one = kept(u1, k)
            two = kept(u2, k)
            base = source(r, s, h)
            three = solve(
                e,
                [
                    z + (GAMMA * C[1]) * a + (GAMMA * C[2]) * b
                    for z, a, b in zip(base, one, two)
                ],
            )
            four = solve(
                e,
                [
                    z + (GAMMA * C[3]) * a + (GAMMA * C[4]) * b + (GAMMA * C[5]) * c
                    for z, a, b, c in zip(base, one, two, three)
                ],
            )
            stiff = flags_ref[lanes(h)].reshape(1, 128) == 1
            put_state(
                y,
                r,
                s,
                h,
                [
                    jnp.where(
                        stiff,
                        z
                        + (SCALED * M[0]) * a
                        + (SCALED * M[1]) * b
                        + (SCALED * M[2]) * c
                        + (SCALED * M[3]) * d,
                        x,
                    )
                    for z, a, b, c, d, x in zip(
                        spread(y0, r, s, h), one, two, three, four, kept(explicit, k)
                    )
                ],
            )
        here = slice(s * LONG, (s + 1) * LONG)
        n = min(LONG, SPEC - s * LONG)
        done = jnp.concatenate([y[0, here, :], y[1, here, :]], axis=1)
        advanced_ref[s * LONG : s * LONG + n, :] = done[:n]
        at_faces = sum(dot(p, hot) for p in split3(done))
        for r in range(2):
            face[r, here, :] = at_faces[:, r * FACES : (r + 1) * FACES]

        if s == 0:
            pl.semaphore_wait(barrier, has_up.astype(I32) + has_down.astype(I32))

        @pl.when(has_down)
        def _(s=s):
            neighbour(0, s, down).start()

        @pl.when(has_up)
        def _(s=s):
            neighbour(1, s, up).start()

    for r, there, other in ((0, has_down, down), (1, has_up, up)):

        @pl.when(there)
        def _(r=r, other=other):
            for s in range(2):
                neighbour(1 - r, s, other).wait_recv()
                here = slice(s * LONG, min(SPEC, (s + 1) * LONG))
                jump_ref[here, r, :] = received[r, here, :] - face[r, here, :]
            for s in range(2):
                neighbour(r, s, other).wait_send()

        @pl.when(jnp.logical_not(there))
        def _(r=r):
            jump_ref[:, r, :] = 0.0 - face[r, :SPEC, :]


def on_device(*args):
    args = [pltpu.with_memory_space_constraint(x, pltpu.HBM) for x in args]
    half = (2, STATE_ROWS, 128)
    chunks = len(CHUNKS)
    return pl.pallas_call(
        kernel,
        out_shape=(
            jax.ShapeDtypeStruct((SPEC, CELLS), F32),
            jax.ShapeDtypeStruct((SPEC, 2, FACES), F32),
        ),
        in_specs=[pl.BlockSpec(memory_space=pltpu.HBM)] * 7,
        out_specs=[pl.BlockSpec(memory_space=pltpu.VMEM)] * 2,
        scratch_shapes=[
            pltpu.VMEM((SPEC, CELLS), F32),
            pltpu.VMEM((CELLS,), I32),
            pltpu.VMEM((2, NR), I32),
            pltpu.VMEM((NR,), F32),
            pltpu.VMEM((NR,), F32),
            pltpu.VMEM((SPEC, NR), F32),
            pltpu.VMEM((2, FACES), I32),
            pltpu.SemaphoreType.DMA((7,)),
            pltpu.VMEM((2, 2 * LONG, FACES), F32),
            pltpu.VMEM((2, 2 * LONG, FACES), F32),
            pltpu.SemaphoreType.DMA((2, 2)),
            pltpu.SemaphoreType.DMA((2, 2)),
            pltpu.VMEM((8, FAC_ROWS), F32),
            pltpu.VMEM((FAC_ROWS, 8), F32),
            pltpu.VMEM((2, RATE_ROWS, 128), I32),
            pltpu.VMEM((2, RATE_ROWS, 128), F32),
            pltpu.VMEM(half, F32),
            pltpu.VMEM(half, F32),
            pltpu.VMEM((2,) + half, F32),
            pltpu.VMEM((2 * S_ROWS, MAIN), BF),
            pltpu.VMEM((S_ROWS, 128), BF),
            pltpu.VMEM((S_ROWS, 128), F32),
            pltpu.VMEM((TRIO_ROWS, 256), F32),
            pltpu.VMEM((RATE_ROWS, CELLS), BF),
            pltpu.VMEM((RATE_ROWS, CELLS), BF),
            pltpu.VMEM((2, FAC_ROWS, CELLS), BF),
            pltpu.VMEM((2, 16 * JAC_ROWS, 128), F32),
            pltpu.VMEM((chunks, BS, BS, 8, 128), F32),
            pltpu.VMEM((chunks, BS, 8, 128), F32),
            pltpu.VMEM((chunks, BS, 8, 128), F32),
            pltpu.VMEM((chunks, BS, 8, 128), F32),
        ],
        compiler_params=pltpu.CompilerParams(
            vmem_limit_bytes=32 * 1024 * 1024, collective_id=0, has_side_effects=True
        ),
        cost_estimate=pl.CostEstimate(
            flops=4_000_000_000, bytes_accessed=3_000_000, transcendentals=400_000
        ),
    )(*args)


def solution(mesh):
    cells = P(None, ("grp", "dev"))
    return jax.shard_map(
        on_device,
        mesh=mesh,
        in_specs=(cells, P(("grp", "dev")), P(), P(), P(), P(), cells),
        out_specs=(cells, P(None, None, ("grp", "dev"))),
        check_vma=False,
    )
```

```python
import jax
import jax.numpy as jnp
from jax import lax
from jax.experimental import pallas as pl
from jax.experimental.pallas import tpu as pltpu
from jax.sharding import PartitionSpec as P

NB = 43
BS = 6
RPB = 36
SPEC = 258
NR = 1548
CELLS = 256
FACES = 128

TRIO = 3
TRIOS = 15
TRIO_STATE = TRIO * BS
TRIO_RATES = TRIO * RPB
TRIO_ROWS = 24
JAC_ROWS = BS * TRIO_ROWS
PITCH = JAC_ROWS + 2
LONG = 8 * TRIO_STATE
STATE_ROWS = 2 * LONG + 8
RATE_ROWS = 1552
FAC_ROWS = 1664
S_ROWS = 272
MAIN = 1536
HALF = MAIN // 2
SPREAD = 144
EARLY = 4 * SPREAD

TIME_STEP = 0.01
GAMMA = 0.5
SCALED = TIME_STEP * GAMMA
A = (2.0, 1.867943637803922, 0.2344449711399156)
C = (
    -7.13761503641231,
    2.580708087951457,
    0.6515950076447975,
    -2.137148994382534,
    -0.3214669691237626,
    -0.6949742501781779,
)
M = (2.255570073418735, 0.2870493262186792, 0.435317943184018, 1.093502252409163)

BF = jnp.bfloat16
F32 = jnp.float32
I32 = jnp.int32
MESH = pl.DeviceIdType.MESH

ROW_GATHER = lax.GatherDimensionNumbers(
    offset_dims=(),
    collapsed_slice_dims=(0,),
    start_index_map=(0,),
    operand_batching_dims=(1,),
    start_indices_batching_dims=(1,),
)


LANE_GATHER = lax.GatherDimensionNumbers(
    offset_dims=(),
    collapsed_slice_dims=(1,),
    start_index_map=(1,),
    operand_batching_dims=(0,),
    start_indices_batching_dims=(0,),
)


def dot(a, b):
    return jnp.dot(a, b, preferred_element_type=F32)


def split2(x):
    hi = x.astype(BF)
    return hi, (x - hi.astype(F32)).astype(BF)


def split3(x):
    hi = x.astype(BF)
    rest = x - hi.astype(F32)
    mid = rest.astype(BF)
    return hi, mid, (rest - mid.astype(F32)).astype(BF)


def take_rows(x, index):
    return lax.gather(
        x,
        index[..., None],
        ROW_GATHER,
        slice_sizes=(1, 1),
        mode=lax.GatherScatterMode.PROMISE_IN_BOUNDS,
    )


def take_lanes(x, index):
    return lax.gather(
        x,
        index[..., None],
        LANE_GATHER,
        slice_sizes=(1, 1),
        mode=lax.GatherScatterMode.PROMISE_IN_BOUNDS,
    )


def factor(e):
    for p in range(BS):
        inverse = 1.0 / e[p][p]
        e[p][p] = inverse
        for t in range(p + 1, BS):
            e[t][p] = e[t][p] * inverse
            for c in range(p + 1, BS):
                e[t][c] = e[t][c] - e[t][p] * e[p][c]
    return e


def solve(e, b):
    x = list(b)
    for t in range(BS):
        for c in range(t):
            x[t] = x[t] - e[t][c] * x[c]
    for t in reversed(range(BS)):
        for c in range(t + 1, BS):
            x[t] = x[t] - e[t][c] * x[c]
        x[t] = x[t] * e[t][t]
    return x


def both(a, b):
    return jnp.concatenate([a, b], axis=0)


def lanes(h):
    return slice(h * 128, (h + 1) * 128)


CHUNKS = [(r, s, h) for s in range(2) for h in range(2) for r in range(TRIO)]


def kernel(
    state_hbm,
    flags_hbm,
    reactants_hbm,
    frequency_hbm,
    barrier_hbm,
    stoich_hbm,
    faces_hbm,
    advanced_ref,
    jump_ref,
    state_ref,
    flags_ref,
    reactants_ref,
    frequency_ref,
    barrier_ref,
    stoich_ref,
    faces_ref,
    in_sem,
    face,
    received,
    send_sem,
    recv_sem,
    rows,
    columns,
    whole,
    index,
    coef,
    y0,
    y,
    part,
    s_split,
    s_tail,
    tail,
    trio,
    r_hi,
    r_lo,
    fac,
    jac,
    lu,
    u1,
    u2,
    explicit,
):
    me = lax.axis_index("dev")
    count = lax.axis_size("dev")
    up = lax.rem(me + 1, count)
    down = lax.rem(me + count - 1, count)
    has_up = me < count - 1
    has_down = me > 0
    barrier = pltpu.get_barrier_semaphore()

    def greet(other):
        pl.semaphore_signal(barrier, inc=1, device_id={"dev": other}, device_id_type=MESH)

    @pl.when(has_up)
    def _():
        greet(up)

    @pl.when(has_down)
    def _():
        greet(down)

    loads = [
        pltpu.make_async_copy(src, dst, in_sem.at[k])
        for k, (src, dst) in enumerate(
            [
                (reactants_hbm, reactants_ref),
                (frequency_hbm, frequency_ref),
                (barrier_hbm, barrier_ref),
                (state_hbm, state_ref),
                (stoich_hbm, stoich_ref),
                (flags_hbm, flags_ref),
                (faces_hbm, faces_ref),
            ]
        )
    ]
    for load in loads:
        load.start()

    rows[...] = jnp.zeros_like(rows)
    tail[...] = jnp.zeros_like(tail)
    jac[:, TRIOS * PITCH :, :] = jnp.zeros((2, PITCH, 128), F32)
    y0[:, SPEC // 8 * 8 :, :] = jnp.zeros((2, STATE_ROWS - SPEC // 8 * 8, 128), F32)
    part[:, :, :, S_ROWS:, :] = jnp.zeros((2, 4, 2, STATE_ROWS - S_ROWS, 128), F32)
    fac[:, RATE_ROWS:, :] = jnp.zeros((2, FAC_ROWS - RATE_ROWS, CELLS), BF)
    for load in loads[:3]:
        load.wait()

    reactants = reactants_ref[...]
    first = ((lax.broadcasted_iota(I32, (2, NR), 1) * 1821) >> 16) * BS
    for k, ref in ((0, frequency_ref), (3, barrier_ref)):
        for q, piece in enumerate(split3(ref[...].reshape(1, NR))):
            rows[k + q : k + q + 1, :NR] = piece.astype(F32)
    rows[6:8, :NR] = (reactants - first).astype(F32)
    whole[...] = jnp.zeros_like(whole)
    whole[0:2, :NR] = reactants
    columns[...] = jnp.transpose(rows[...]).astype(BF)
    row = lax.broadcasted_iota(I32, (8, 512), 0)
    col = lax.broadcasted_iota(I32, (8, 512), 1)
    pick = (row >= 3).astype(I32) + (row >= 6).astype(I32) + (row >= 7).astype(I32)
    pick = (pick == (col >> 7)).astype(F32).astype(BF)
    loads[3].wait()

    for h in range(2):
        y0[h, :SPEC, :] = state_ref[:, lanes(h)]

    sub = lax.broadcasted_iota(I32, (8, 128), 0)

    def reactant(ref, h, at, want):
        one = at // RPB
        two = min((at + 7) // RPB, NB - 1)
        got = take_rows(ref[h, one * BS : one * BS + 8, :], want)
        if two != one:
            other = take_rows(ref[h, two * BS : two * BS + 8, :], want)
            got = jnp.where(sub < two * RPB - at, got, other)
        return got

    def put_rates(at, h, values):
        hi, lo = split2(both(*values))
        r_hi[at : at + 16, lanes(h)] = hi
        r_lo[at : at + 16, lanes(h)] = lo

    theta = 1.0 - 1.0 / state_ref[SPEC - 1 : SPEC, :]
    def begin(at, wide):
        wants, freq, ener = [], [], []
        for k in (at, at + 8):
            own = wide[k % SPREAD : k % SPREAD + 8, :]
            freq.append(own[:, :128])
            ener.append(own[:, 128:256])
            want = [own[:, 256 + w * 128 : 384 + w * 128].astype(I32) for w in range(2)]
            for w in range(2):
                index[w, k : k + 8, :] = want[w]
            wants.append(want)
        for h in range(2):
            one, two, rate = [], [], []
            for q, k in enumerate((at, at + 8)):
                c = freq[q] * jnp.exp(ener[q] * theta[:, lanes(h)])
                coef[h, k : k + 8, :] = c
                former = reactant(y0, h, k, wants[q][0])
                latter = reactant(y0, h, k, wants[q][1])
                one.append(c * latter)
                two.append(c * former)
                rate.append(one[-1] * former)
            fac[0, at : at + 16, lanes(h)] = both(*one).astype(BF)
            fac[1, at : at + 16, lanes(h)] = both(*two).astype(BF)
            put_rates(at, h, rate)

    def split_stoichiometry(k):
        span = slice(k * HALF, (k + 1) * HALF)
        for at in range(0, SPEC, 16):
            n = min(16, SPEC - at)
            x = stoich_ref[at : at + n, span]
            if n < 16:
                x = both(x, jnp.zeros((16 - n, HALF), F32))
            hi, lo = split2(x)
            s_split[at : at + 16, span] = hi
            s_split[S_ROWS + at : S_ROWS + at + 16, span] = lo

    def split_tail():
        tail[:SPEC, : NR - MAIN] = stoich_ref[:, MAIN:]
        for at in range(0, S_ROWS, 16):
            x = tail[at : at + 16, :]
            hi = x.astype(BF).astype(F32)
            lo = x - hi
            s_tail[at : at + 16, :] = (
                hi + pltpu.roll(lo, 16, 1) + pltpu.roll(hi, 32, 1)
            ).astype(BF)

    def source_part(stage, k):
        low, mid, near, high = (k * HALF + q for q in (0, 512, 256, 768))
        long = dot(s_split[:, low:mid], r_hi[low:mid, :])
        one = long[:S_ROWS] + long[S_ROWS:] + dot(s_split[:S_ROWS, low:near], r_lo[low:near, :])
        long = dot(s_split[:, mid:high], r_hi[mid:high, :])
        two = long[:S_ROWS] + long[S_ROWS:] + dot(s_split[:S_ROWS, near:high], r_lo[near:high, :])
        if k == 1:
            last = jnp.concatenate([r_hi[MAIN:, :], r_hi[MAIN:, :], r_lo[MAIN:, :]], axis=0)
            two = two + dot(s_tail[:, :48], last)
        for q, total in enumerate((one, two)):
            for h in range(2):
                part[stage % 2, 2 * k + q, h, :S_ROWS, :] = total[:, lanes(h)]

    def again(at):
        wants = [[index[w, k : k + 8, :] for w in range(2)] for k in (at, at + 8)]
        for h in range(2):
            put_rates(
                at,
                h,
                [
                    coef[h, k : k + 8, :] * reactant(y, h, k, want[0]) * reactant(y, h, k, want[1])
                    for k, want in zip((at, at + 8), wants)
                ],
            )

    def state_rows(r, s, m):
        return pl.ds(s * LONG + r * BS + m, 8, stride=TRIO_STATE)

    def spread(ref, r, s, h):
        return [ref[h, state_rows(r, s, m), :] for m in range(BS)]

    def source(stage, r, s, h):
        own = part.at[stage % 2]
        return [
            (own[0, h, state_rows(r, s, m), :] + own[1, h, state_rows(r, s, m), :])
            + (own[2, h, state_rows(r, s, m), :] + own[3, h, state_rows(r, s, m), :])
            for m in range(BS)
        ]

    def put_state(ref, r, s, h, values):
        for m in range(BS):
            ref[h, state_rows(r, s, m), :] = values[m]

    def keep(ref, k, values):
        for m in range(BS):
            ref[k, m] = values[m]

    def kept(ref, k):
        return [ref[k, m] for m in range(BS)]

    def factors(k):
        return [[lu[k, i, m] for m in range(BS)] for i in range(BS)]

    shift = ((lax.broadcasted_iota(I32, (TRIO_ROWS, 1), 0) * 43) >> 8) * BS
    def jacobian(t):
        start = t * TRIO_RATES // 16 * 16
        low = start // 128 * 128
        top = t * TRIO_STATE
        n = min(TRIO_STATE, SPEC - top)
        wide = min(256, NR - low)
        if wide < 256 or n < TRIO_STATE:
            trio[t] = jnp.zeros((TRIO_ROWS, 256), F32)
        trio[t, :n, :wide] = stoich_ref[top : top + n, low : low + wide] * -SCALED
        x = trio[t]
        reacts = whole[:, low : low + 256]
        if start > low:
            x = pltpu.roll(x, 256 - (start - low), 1)
            reacts = pltpu.roll(reacts, 256 - (start - low), 1)
        x = x[:, :128]
        reacts = reacts[:, :128]
        sides = []
        for w in range(2):
            where = reacts[w : w + 1, :] - (shift + top)
            sides.append(
                jnp.concatenate([jnp.where(where == m, x, 0.0) for m in range(BS)], axis=0)
            )
        coupling = jnp.concatenate([side.astype(BF) for side in sides], axis=1)
        factors_here = both(fac[0, start : start + 128, :], fac[1, start : start + 128, :])
        block = dot(coupling, factors_here)
        for h in range(2):
            jac[h, t * PITCH : t * PITCH + JAC_ROWS, :] = block[:, lanes(h)]

    def eliminate(s):
        for k, (r, s_k, h) in enumerate(CHUNKS):
            if s_k != s:
                continue
            e = [
                [
                    jac[h, pl.ds(s * 8 * PITCH + m * TRIO_ROWS + r * BS + i, 8, stride=PITCH), :]
                    for m in range(BS)
                ]
                for i in range(BS)
            ]
            for i in range(BS):
                e[i][i] = 1.0 + e[i][i]
            e = factor(e)
            for i in range(BS):
                for m in range(BS):
                    lu[k, i, m] = e[i][m]

    def first_stage(k, r, s, h):
        rhs = source(0, r, s, h)
        x = solve(factors(k), rhs)
        start = spread(y0, r, s, h)
        keep(u1, k, x)
        keep(explicit, k, [a + TIME_STEP * b for a, b in zip(start, rhs)])
        put_state(y, r, s, h, [a + (SCALED * A[0]) * b for a, b in zip(start, x)])

    def second_stage(k, r, s, h):
        one = kept(u1, k)
        x = solve(factors(k), [a + (GAMMA * C[0]) * b for a, b in zip(source(1, r, s, h), one)])
        keep(u2, k, x)
        put_state(
            y,
            r,
            s,
            h,
            [
                a + (SCALED * A[1]) * b + (SCALED * A[2]) * c
                for a, b, c in zip(spread(y0, r, s, h), one, x)
            ],
        )

    def next_source(stage, step):
        for half in range(2):
            for k, (r, s, h) in enumerate(CHUNKS):
                if s == half:
                    step(k, r, s, h)
            for at in range(half * HALF, HALF if half == 0 else RATE_ROWS, 16):
                again(at)
            source_part(stage, half)

    for at in range(0, RATE_ROWS, 16):
        if at % SPREAD == 0:
            wide = dot(columns[at : min(at + SPREAD, RATE_ROWS), :], pick)
        if at == EARLY:
            for load in loads[4:]:
                load.wait()
        begin(at, wide)
        if at + 16 == HALF:
            split_stoichiometry(0)
            source_part(0, 0)
    split_stoichiometry(1)
    split_tail()
    for t in range(8):
        jacobian(t)
    source_part(0, 1)
    for t in range(8, TRIOS):
        jacobian(t)
    eliminate(0)
    eliminate(1)

    next_source(1, first_stage)
    next_source(2, second_stage)

    cells = [jnp.broadcast_to(faces_ref[r : r + 1, :], (8, FACES)) for r in range(2)]
    near = [c < 128 for c in cells]
    cells = [c & 127 for c in cells]

    def neighbour(r, s, other):
        here = pl.ds(s * LONG, LONG)
        return pltpu.make_async_remote_copy(
            src_ref=face.at[r, here],
            dst_ref=received.at[1 - r, here],
            send_sem=send_sem.at[r, s],
            recv_sem=recv_sem.at[1 - r, s],
            device_id={"dev": other},
            device_id_type=MESH,
        )

    for s in range(2):
        for k, (r, s_k, h) in enumerate(CHUNKS):
            if s_k != s:
                continue
            e = factors(k)
            one = kept(u1, k)
            two = kept(u2, k)
            base = source(2, r, s, h)
            three = solve(
                e,
                [
                    z + (GAMMA * C[1]) * a + (GAMMA * C[2]) * b
                    for z, a, b in zip(base, one, two)
                ],
            )
            rest = solve(
                e,
                [
                    (M[2] + M[3]) * z
                    + (GAMMA * (M[2] * C[1] + M[3] * C[3])) * a
                    + (GAMMA * (M[2] * C[2] + M[3] * C[4])) * b
                    + (GAMMA * M[3] * C[5]) * c
                    for z, a, b, c in zip(base, one, two, three)
                ],
            )
            stiff = flags_ref[lanes(h)].reshape(1, 128) == 1
            put_state(
                y,
                r,
                s,
                h,
                [
                    jnp.where(
                        stiff,
                        z + (SCALED * M[0]) * a + (SCALED * M[1]) * b + SCALED * d,
                        x,
                    )
                    for z, a, b, d, x in zip(
                        spread(y0, r, s, h), one, two, rest, kept(explicit, k)
                    )
                ],
            )
        here = slice(s * LONG, (s + 1) * LONG)
        n = min(LONG, SPEC - s * LONG)
        done = jnp.concatenate([y[0, here, :], y[1, here, :]], axis=1)
        advanced_ref[s * LONG : s * LONG + n, :] = done[:n]
        for at in range(s * LONG, (s + 1) * LONG, 8):
            halves = [y[h, at : at + 8, :] for h in range(2)]
            for r in range(2):
                face[r, at : at + 8, :] = jnp.where(
                    near[r], take_lanes(halves[0], cells[r]), take_lanes(halves[1], cells[r])
                )

        if s == 0:
            pl.semaphore_wait(barrier, has_up.astype(I32) + has_down.astype(I32))

        @pl.when(has_down)
        def _(s=s):
            neighbour(0, s, down).start()

        @pl.when(has_up)
        def _(s=s):
            neighbour(1, s, up).start()

    for r, there, other in ((0, has_down, down), (1, has_up, up)):

        @pl.when(there)
        def _(r=r, other=other):
            for s in range(2):
                neighbour(1 - r, s, other).wait_recv()
                n = min(SPEC - s * LONG, LONG)
                here = slice(s * LONG, s * LONG + n)
                jump_ref[r, here, :] = received[r, here, :] - face[r, here, :]
            for s in range(2):
                neighbour(r, s, other).wait_send()

        @pl.when(jnp.logical_not(there))
        def _(r=r):
            jump_ref[r] = 0.0 - face[r, :SPEC, :]


def write(advanced, jump, advanced_hbm, jump_hbm, sem):
    copies = [
        pltpu.make_async_copy(advanced, advanced_hbm, sem.at[0]),
        pltpu.make_async_copy(jump.at[0], jump_hbm.at[:, 0, :], sem.at[1]),
        pltpu.make_async_copy(jump.at[1], jump_hbm.at[:, 1, :], sem.at[2]),
    ]
    for copy in copies:
        copy.start()
    for copy in copies:
        copy.wait()


def on_device(*args):
    args = [pltpu.with_memory_space_constraint(x, pltpu.HBM) for x in args]
    half = (2, STATE_ROWS, 128)
    chunks = len(CHUNKS)
    advanced, jump = pl.pallas_call(
        kernel,
        out_shape=(
            jax.ShapeDtypeStruct((SPEC, CELLS), F32),
            jax.ShapeDtypeStruct((2, SPEC, FACES), F32),
        ),
        in_specs=[pl.BlockSpec(memory_space=pltpu.HBM)] * 7,
        out_specs=[pl.BlockSpec(memory_space=pltpu.VMEM)] * 2,
        scratch_shapes=[
            pltpu.VMEM((SPEC, CELLS), F32),
            pltpu.VMEM((CELLS,), I32),
            pltpu.VMEM((2, NR), I32),
            pltpu.VMEM((NR,), F32),
            pltpu.VMEM((NR,), F32),
            pltpu.VMEM((SPEC, NR), F32),
            pltpu.VMEM((2, FACES), I32),
            pltpu.SemaphoreType.DMA((7,)),
            pltpu.VMEM((2, 2 * LONG, FACES), F32),
            pltpu.VMEM((2, 2 * LONG, FACES), F32),
            pltpu.SemaphoreType.DMA((2, 2)),
            pltpu.SemaphoreType.DMA((2, 2)),
            pltpu.VMEM((8, FAC_ROWS), F32),
            pltpu.VMEM((FAC_ROWS, 8), BF),
            pltpu.VMEM((8, FAC_ROWS), I32),
            pltpu.VMEM((2, RATE_ROWS, 128), I32),
            pltpu.VMEM((2, RATE_ROWS, 128), F32),
            pltpu.VMEM(half, F32),
            pltpu.VMEM(half, F32),
            pltpu.VMEM((2, 4) + half, F32),
            pltpu.VMEM((2 * S_ROWS, MAIN), BF),
            pltpu.VMEM((S_ROWS, 128), BF),
            pltpu.VMEM((S_ROWS, 128), F32),
            pltpu.VMEM((TRIOS, TRIO_ROWS, 256), F32),
            pltpu.VMEM((RATE_ROWS, CELLS), BF),
            pltpu.VMEM((RATE_ROWS, CELLS), BF),
            pltpu.VMEM((2, FAC_ROWS, CELLS), BF),
            pltpu.VMEM((2, 16 * PITCH, 128), F32),
            pltpu.VMEM((chunks, BS, BS, 8, 128), F32),
            pltpu.VMEM((chunks, BS, 8, 128), F32),
            pltpu.VMEM((chunks, BS, 8, 128), F32),
            pltpu.VMEM((chunks, BS, 8, 128), F32),
        ],
        compiler_params=pltpu.CompilerParams(
            vmem_limit_bytes=32 * 1024 * 1024, collective_id=0, has_side_effects=True
        ),
        cost_estimate=pl.CostEstimate(
            flops=4_000_000_000, bytes_accessed=3_000_000, transcendentals=400_000
        ),
    )(*args)
    return pl.pallas_call(
        write,
        out_shape=(
            jax.ShapeDtypeStruct((SPEC, CELLS), F32),
            jax.ShapeDtypeStruct((SPEC, 2, FACES), F32),
        ),
        in_specs=[pl.BlockSpec(memory_space=pltpu.VMEM)] * 2,
        out_specs=[pl.BlockSpec(memory_space=pltpu.HBM)] * 2,
        scratch_shapes=[pltpu.SemaphoreType.DMA((3,))],
        compiler_params=pltpu.CompilerParams(vmem_limit_bytes=32 * 1024 * 1024),
    )(advanced, jump)


def solution(mesh):
    cells = P(None, ("grp", "dev"))
    return jax.shard_map(
        on_device,
        mesh=mesh,
        in_specs=(cells, P(("grp", "dev")), P(), P(), P(), P(), cells),
        out_specs=(cells, P(None, None, ("grp", "dev"))),
        check_vma=False,
    )
```

```python
import jax
import jax.numpy as jnp
from jax import lax
from jax.experimental import pallas as pl
from jax.experimental.pallas import tpu as pltpu
from jax.sharding import PartitionSpec as P

NB = 43
BS = 6
RPB = 36
SPEC = 258
NR = 1548
CELLS = 256
FACES = 128

TRIO = 3
TRIOS = 15
TRIO_STATE = TRIO * BS
TRIO_RATES = TRIO * RPB
TRIO_ROWS = 24
JAC_ROWS = BS * TRIO_ROWS
PITCH = JAC_ROWS + 2
LONG = 8 * TRIO_STATE
STATE_ROWS = 2 * LONG + 8
RATE_ROWS = 1552
FAC_ROWS = 1664
S_ROWS = 272
MAIN = 1536
HALF = MAIN // 2
FACE_ROWS = 264
SPREAD = 144
EARLY = 4 * SPREAD

TIME_STEP = 0.01
GAMMA = 0.5
SCALED = TIME_STEP * GAMMA
A = (2.0, 1.867943637803922, 0.2344449711399156)
C = (
    -7.13761503641231,
    2.580708087951457,
    0.6515950076447975,
    -2.137148994382534,
    -0.3214669691237626,
    -0.6949742501781779,
)
M = (2.255570073418735, 0.2870493262186792, 0.435317943184018, 1.093502252409163)

BF = jnp.bfloat16
F32 = jnp.float32
I32 = jnp.int32
MESH = pl.DeviceIdType.MESH

ROW_GATHER = lax.GatherDimensionNumbers(
    offset_dims=(),
    collapsed_slice_dims=(0,),
    start_index_map=(0,),
    operand_batching_dims=(1,),
    start_indices_batching_dims=(1,),
)


LANE_GATHER = lax.GatherDimensionNumbers(
    offset_dims=(),
    collapsed_slice_dims=(1,),
    start_index_map=(1,),
    operand_batching_dims=(0,),
    start_indices_batching_dims=(0,),
)


def dot(a, b):
    return jnp.dot(a, b, preferred_element_type=F32)


def split2(x):
    hi = x.astype(BF)
    return hi, (x - hi.astype(F32)).astype(BF)


def split3(x):
    hi = x.astype(BF)
    rest = x - hi.astype(F32)
    mid = rest.astype(BF)
    return hi, mid, (rest - mid.astype(F32)).astype(BF)


def take_rows(x, index):
    return lax.gather(
        x,
        index[..., None],
        ROW_GATHER,
        slice_sizes=(1, 1),
        mode=lax.GatherScatterMode.PROMISE_IN_BOUNDS,
    )


def take_lanes(x, index):
    return lax.gather(
        x,
        index[..., None],
        LANE_GATHER,
        slice_sizes=(1, 1),
        mode=lax.GatherScatterMode.PROMISE_IN_BOUNDS,
    )


def factor(e):
    for p in range(BS):
        inverse = 1.0 / e[p][p]
        e[p][p] = inverse
        for t in range(p + 1, BS):
            e[t][p] = e[t][p] * inverse
            for c in range(p + 1, BS):
                e[t][c] = e[t][c] - e[t][p] * e[p][c]
    return e


def solve(e, b):
    x = list(b)
    for t in range(BS):
        for c in range(t):
            x[t] = x[t] - e[t][c] * x[c]
    for t in reversed(range(BS)):
        for c in range(t + 1, BS):
            x[t] = x[t] - e[t][c] * x[c]
        x[t] = x[t] * e[t][t]
    return x


def both(a, b):
    return jnp.concatenate([a, b], axis=0)


def lanes(h):
    return slice(h * 128, (h + 1) * 128)


CHUNKS = [(r, s, h) for s in range(2) for h in range(2) for r in range(TRIO)]


def kernel(
    state_hbm,
    flags_hbm,
    reactants_hbm,
    frequency_hbm,
    barrier_hbm,
    stoich_hbm,
    faces_hbm,
    advanced_ref,
    jump_ref,
    state_ref,
    flags_ref,
    reactants_ref,
    frequency_ref,
    barrier_ref,
    stoich_ref,
    faces_ref,
    in_sem,
    face,
    received,
    send_sem,
    recv_sem,
    rows,
    columns,
    whole,
    spots,
    index,
    coef,
    y0,
    y,
    part,
    s_split,
    s_tail,
    tail,
    trio,
    r_hi,
    r_lo,
    fac,
    jac,
    lu,
    u1,
    u2,
    explicit,
):
    me = lax.axis_index("dev")
    count = lax.axis_size("dev")
    up = lax.rem(me + 1, count)
    down = lax.rem(me + count - 1, count)
    has_up = me < count - 1
    has_down = me > 0
    barrier = pltpu.get_barrier_semaphore()

    def greet(other):
        pl.semaphore_signal(barrier, inc=1, device_id={"dev": other}, device_id_type=MESH)

    @pl.when(has_up)
    def _():
        greet(up)

    @pl.when(has_down)
    def _():
        greet(down)

    loads = [
        pltpu.make_async_copy(src, dst, in_sem.at[k])
        for k, (src, dst) in enumerate(
            [
                (reactants_hbm, reactants_ref),
                (frequency_hbm, frequency_ref),
                (barrier_hbm, barrier_ref),
                (state_hbm, state_ref),
                (stoich_hbm, stoich_ref),
                (flags_hbm, flags_ref),
                (faces_hbm, faces_ref),
            ]
        )
    ]
    for load in loads:
        load.start()

    rows[...] = jnp.zeros_like(rows)
    tail[...] = jnp.zeros_like(tail)
    jac[:, TRIOS * PITCH :, :] = jnp.zeros((2, PITCH, 128), F32)
    y0[:, SPEC // 8 * 8 :, :] = jnp.zeros((2, STATE_ROWS - SPEC // 8 * 8, 128), F32)
    part[:, :, :, S_ROWS:, :] = jnp.zeros((2, 4, 2, STATE_ROWS - S_ROWS, 128), F32)
    fac[:, RATE_ROWS:, :] = jnp.zeros((2, FAC_ROWS - RATE_ROWS, CELLS), BF)
    for load in loads[:3]:
        load.wait()

    reactants = reactants_ref[...]
    first = ((lax.broadcasted_iota(I32, (2, NR), 1) * 1821) >> 16) * BS
    for k, ref in ((0, frequency_ref), (3, barrier_ref)):
        for q, piece in enumerate(split3(ref[...].reshape(1, NR))):
            rows[k + q : k + q + 1, :NR] = piece.astype(F32)
    whole[...] = jnp.zeros_like(whole)
    whole[0:2, :NR] = reactants
    whole[2:4, :NR] = reactants - first
    spots[...] = jnp.transpose(whole[...])
    columns[...] = jnp.transpose(rows[...]).astype(BF)
    row = lax.broadcasted_iota(I32, (8, 256), 0)
    col = lax.broadcasted_iota(I32, (8, 256), 1)
    pick = ((row >= 3) == (col >= 128)).astype(F32).astype(BF)
    loads[3].wait()

    for h in range(2):
        y0[h, :SPEC, :] = state_ref[:, lanes(h)]

    sub = lax.broadcasted_iota(I32, (8, 128), 0)

    def reactant(ref, h, at, want):
        one = at // RPB
        two = min((at + 7) // RPB, NB - 1)
        got = take_rows(ref[h, one * BS : one * BS + 8, :], want)
        if two != one:
            other = take_rows(ref[h, two * BS : two * BS + 8, :], want)
            got = jnp.where(sub < two * RPB - at, got, other)
        return got

    def put_rates(at, h, values):
        hi, lo = split2(both(*values))
        r_hi[at : at + 16, lanes(h)] = hi
        r_lo[at : at + 16, lanes(h)] = lo

    theta = 1.0 - 1.0 / state_ref[SPEC - 1 : SPEC, :]
    def begin(at, wide):
        wants, freq, ener = [], [], []
        for k in (at, at + 8):
            own = wide[k % SPREAD : k % SPREAD + 8, :]
            freq.append(own[:, :128])
            ener.append(own[:, 128:256])
            want = [
                jnp.broadcast_to(spots[k : k + 8, 2 + w : 3 + w], (8, 128)) for w in range(2)
            ]
            for w in range(2):
                index[w, k : k + 8, :] = want[w]
            wants.append(want)
        for h in range(2):
            one, two, rate = [], [], []
            for q, k in enumerate((at, at + 8)):
                c = freq[q] * jnp.exp(ener[q] * theta[:, lanes(h)])
                coef[h, k : k + 8, :] = c
                former = reactant(y0, h, k, wants[q][0])
                latter = reactant(y0, h, k, wants[q][1])
                one.append(c * latter)
                two.append(c * former)
                rate.append(one[-1] * former)
            fac[0, at : at + 16, lanes(h)] = both(*one).astype(BF)
            fac[1, at : at + 16, lanes(h)] = both(*two).astype(BF)
            put_rates(at, h, rate)

    def split_stoichiometry(k):
        span = slice(k * HALF, (k + 1) * HALF)
        for at in range(0, SPEC, 16):
            n = min(16, SPEC - at)
            x = stoich_ref[at : at + n, span]
            if n < 16:
                x = both(x, jnp.zeros((16 - n, HALF), F32))
            hi, lo = split2(x)
            s_split[at : at + 16, span] = hi
            s_split[S_ROWS + at : S_ROWS + at + 16, span] = lo

    def split_tail():
        tail[:SPEC, : NR - MAIN] = stoich_ref[:, MAIN:]
        for at in range(0, S_ROWS, 16):
            x = tail[at : at + 16, :]
            hi = x.astype(BF).astype(F32)
            lo = x - hi
            s_tail[at : at + 16, :] = (
                hi + pltpu.roll(lo, 16, 1) + pltpu.roll(hi, 32, 1)
            ).astype(BF)

    def source_part(stage, k, top=0, end=S_ROWS):
        low, mid, near, high = (k * HALF + q for q in (0, 512, 256, 768))
        n = end - top

        def stacked(span):
            hi = s_split[top:end, span]
            lo = s_split[S_ROWS + top : S_ROWS + end, span]
            long = dot(both(hi, lo), r_hi[span, :])
            return long[:n] + long[n:]

        def corrected(span):
            return dot(s_split[top:end, span], r_lo[span, :])

        one = stacked(slice(low, mid)) + corrected(slice(low, near))
        two = stacked(slice(mid, high)) + corrected(slice(near, high))
        if k == 1:
            last = jnp.concatenate([r_hi[MAIN:, :], r_hi[MAIN:, :], r_lo[MAIN:, :]], axis=0)
            two = two + dot(s_tail[top:end, :48], last)
        for q, total in enumerate((one, two)):
            for h in range(2):
                part[stage % 2, 2 * k + q, h, top:end, :] = total[:, lanes(h)]

    def again(at):
        wants = [[index[w, k : k + 8, :] for w in range(2)] for k in (at, at + 8)]
        for h in range(2):
            put_rates(
                at,
                h,
                [
                    coef[h, k : k + 8, :] * reactant(y, h, k, want[0]) * reactant(y, h, k, want[1])
                    for k, want in zip((at, at + 8), wants)
                ],
            )

    def state_rows(r, s, m):
        return pl.ds(s * LONG + r * BS + m, 8, stride=TRIO_STATE)

    def spread(ref, r, s, h):
        return [ref[h, state_rows(r, s, m), :] for m in range(BS)]

    def source(stage, r, s, h):
        own = part.at[stage % 2]
        return [
            (own[0, h, state_rows(r, s, m), :] + own[1, h, state_rows(r, s, m), :])
            + (own[2, h, state_rows(r, s, m), :] + own[3, h, state_rows(r, s, m), :])
            for m in range(BS)
        ]

    def put_state(ref, r, s, h, values):
        for m in range(BS):
            ref[h, state_rows(r, s, m), :] = values[m]

    def keep(ref, k, values):
        for m in range(BS):
            ref[k, m] = values[m]

    def kept(ref, k):
        return [ref[k, m] for m in range(BS)]

    def factors(k):
        return [[lu[k, i, m] for m in range(BS)] for i in range(BS)]

    shift = ((lax.broadcasted_iota(I32, (TRIO_ROWS, 1), 0) * 43) >> 8) * BS
    def jacobian(t):
        start = t * TRIO_RATES // 16 * 16
        low = start // 128 * 128
        top = t * TRIO_STATE
        n = min(TRIO_STATE, SPEC - top)
        wide = min(256, NR - low)
        if wide < 256 or n < TRIO_STATE:
            trio[t] = jnp.zeros((TRIO_ROWS, 256), F32)
        trio[t, :n, :wide] = stoich_ref[top : top + n, low : low + wide] * -SCALED
        x = trio[t]
        reacts = whole[:, low : low + 256]
        if start > low:
            x = pltpu.roll(x, 256 - (start - low), 1)
            reacts = pltpu.roll(reacts, 256 - (start - low), 1)
        x = x[:, :128]
        reacts = reacts[:, :128]
        sides = []
        for w in range(2):
            where = reacts[w : w + 1, :] - (shift + top)
            sides.append(
                jnp.concatenate([jnp.where(where == m, x, 0.0) for m in range(BS)], axis=0)
            )
        coupling = jnp.concatenate([side.astype(BF) for side in sides], axis=1)
        factors_here = both(fac[0, start : start + 128, :], fac[1, start : start + 128, :])
        block = dot(coupling, factors_here)
        for h in range(2):
            jac[h, t * PITCH : t * PITCH + JAC_ROWS, :] = block[:, lanes(h)]

    def eliminate(s):
        for k, (r, s_k, h) in enumerate(CHUNKS):
            if s_k != s:
                continue
            e = [
                [
                    jac[h, pl.ds(s * 8 * PITCH + m * TRIO_ROWS + r * BS + i, 8, stride=PITCH), :]
                    for m in range(BS)
                ]
                for i in range(BS)
            ]
            for i in range(BS):
                e[i][i] = 1.0 + e[i][i]
            e = factor(e)
            for i in range(BS):
                for m in range(BS):
                    lu[k, i, m] = e[i][m]

    def first_stage(k, r, s, h):
        rhs = source(0, r, s, h)
        x = solve(factors(k), rhs)
        start = spread(y0, r, s, h)
        keep(u1, k, x)
        keep(explicit, k, [a + TIME_STEP * b for a, b in zip(start, rhs)])
        put_state(y, r, s, h, [a + (SCALED * A[0]) * b for a, b in zip(start, x)])

    def second_stage(k, r, s, h):
        one = kept(u1, k)
        x = solve(factors(k), [a + (GAMMA * C[0]) * b for a, b in zip(source(1, r, s, h), one)])
        keep(u2, k, x)
        put_state(
            y,
            r,
            s,
            h,
            [
                a + (SCALED * A[1]) * b + (SCALED * A[2]) * c
                for a, b, c in zip(spread(y0, r, s, h), one, x)
            ],
        )

    def next_source(stage, step):
        for half in range(2):
            for k, (r, s, h) in enumerate(CHUNKS):
                if s == half:
                    step(k, r, s, h)
            for at in range(half * HALF, HALF if half == 0 else RATE_ROWS, 16):
                again(at)
            if stage == 2 and half == 1:
                source_part(stage, half, 0, LONG)
            else:
                source_part(stage, half)

    for at in range(0, RATE_ROWS, 16):
        if at % SPREAD == 0:
            wide = dot(columns[at : min(at + SPREAD, RATE_ROWS), :], pick)
        if at == EARLY:
            for load in loads[4:]:
                load.wait()
        begin(at, wide)
        if at + 16 == HALF:
            split_stoichiometry(0)
            source_part(0, 0)
    split_stoichiometry(1)
    split_tail()
    for t in range(8):
        jacobian(t)
    source_part(0, 1)
    for t in range(8, TRIOS):
        jacobian(t)
    eliminate(0)
    eliminate(1)

    next_source(1, first_stage)
    next_source(2, second_stage)

    cells = [jnp.broadcast_to(faces_ref[r : r + 1, :], (8, FACES)) for r in range(2)]
    near = [c < 128 for c in cells]
    cells = [c & 127 for c in cells]

    def neighbour(r, s, other):
        here = pl.ds(s * LONG, LONG if s == 0 else FACE_ROWS - LONG)
        return pltpu.make_async_remote_copy(
            src_ref=face.at[r, here],
            dst_ref=received.at[1 - r, here],
            send_sem=send_sem.at[r, s],
            recv_sem=recv_sem.at[1 - r, s],
            device_id={"dev": other},
            device_id_type=MESH,
        )

    for s in range(2):
        if s == 1:
            source_part(2, 1, LONG, S_ROWS)
        for k, (r, s_k, h) in enumerate(CHUNKS):
            if s_k != s:
                continue
            e = factors(k)
            one = kept(u1, k)
            two = kept(u2, k)
            base = source(2, r, s, h)
            three = solve(
                e,
                [
                    z + (GAMMA * C[1]) * a + (GAMMA * C[2]) * b
                    for z, a, b in zip(base, one, two)
                ],
            )
            rest = solve(
                e,
                [
                    (M[2] + M[3]) * z
                    + (GAMMA * (M[2] * C[1] + M[3] * C[3])) * a
                    + (GAMMA * (M[2] * C[2] + M[3] * C[4])) * b
                    + (GAMMA * M[3] * C[5]) * c
                    for z, a, b, c in zip(base, one, two, three)
                ],
            )
            stiff = flags_ref[lanes(h)].reshape(1, 128) == 1
            put_state(
                y,
                r,
                s,
                h,
                [
                    jnp.where(
                        stiff,
                        z + (SCALED * M[0]) * a + (SCALED * M[1]) * b + SCALED * d,
                        x,
                    )
                    for z, a, b, d, x in zip(
                        spread(y0, r, s, h), one, two, rest, kept(explicit, k)
                    )
                ],
            )
        here = slice(s * LONG, (s + 1) * LONG)
        n = min(LONG, SPEC - s * LONG)
        done = jnp.concatenate([y[0, here, :], y[1, here, :]], axis=1)
        advanced_ref[s * LONG : s * LONG + n, :] = done[:n]
        for at in range(s * LONG, LONG if s == 0 else FACE_ROWS, 8):
            halves = [y[h, at : at + 8, :] for h in range(2)]
            for r in range(2):
                face[r, at : at + 8, :] = jnp.where(
                    near[r], take_lanes(halves[0], cells[r]), take_lanes(halves[1], cells[r])
                )

        if s == 0:
            pl.semaphore_wait(barrier, has_up.astype(I32) + has_down.astype(I32))

        @pl.when(has_down)
        def _(s=s):
            neighbour(0, s, down).start()

        @pl.when(has_up)
        def _(s=s):
            neighbour(1, s, up).start()

    for r, there, other in ((0, has_down, down), (1, has_up, up)):

        @pl.when(there)
        def _(r=r, other=other):
            for s in range(2):
                neighbour(1 - r, s, other).wait_recv()
                n = min(SPEC - s * LONG, LONG)
                here = slice(s * LONG, s * LONG + n)
                jump_ref[r, here, :] = received[r, here, :] - face[r, here, :]
            for s in range(2):
                neighbour(r, s, other).wait_send()

        @pl.when(jnp.logical_not(there))
        def _(r=r):
            jump_ref[r] = 0.0 - face[r, :SPEC, :]


def write(advanced, jump, advanced_hbm, jump_hbm, sem):
    copies = [
        pltpu.make_async_copy(advanced, advanced_hbm, sem.at[0]),
        pltpu.make_async_copy(jump.at[0], jump_hbm.at[:, 0, :], sem.at[1]),
        pltpu.make_async_copy(jump.at[1], jump_hbm.at[:, 1, :], sem.at[2]),
    ]
    for copy in copies:
        copy.start()
    for copy in copies:
        copy.wait()


def on_device(*args):
    args = [pltpu.with_memory_space_constraint(x, pltpu.HBM) for x in args]
    half = (2, STATE_ROWS, 128)
    chunks = len(CHUNKS)
    advanced, jump = pl.pallas_call(
        kernel,
        out_shape=(
            jax.ShapeDtypeStruct((SPEC, CELLS), F32),
            jax.ShapeDtypeStruct((2, SPEC, FACES), F32),
        ),
        in_specs=[pl.BlockSpec(memory_space=pltpu.HBM)] * 7,
        out_specs=[pl.BlockSpec(memory_space=pltpu.VMEM)] * 2,
        scratch_shapes=[
            pltpu.VMEM((SPEC, CELLS), F32),
            pltpu.VMEM((CELLS,), I32),
            pltpu.VMEM((2, NR), I32),
            pltpu.VMEM((NR,), F32),
            pltpu.VMEM((NR,), F32),
            pltpu.VMEM((SPEC, NR), F32),
            pltpu.VMEM((2, FACES), I32),
            pltpu.SemaphoreType.DMA((7,)),
            pltpu.VMEM((2, FACE_ROWS, FACES), F32),
            pltpu.VMEM((2, FACE_ROWS, FACES), F32),
            pltpu.SemaphoreType.DMA((2, 2)),
            pltpu.SemaphoreType.DMA((2, 2)),
            pltpu.VMEM((8, FAC_ROWS), F32),
            pltpu.VMEM((FAC_ROWS, 8), BF),
            pltpu.VMEM((8, FAC_ROWS), I32),
            pltpu.VMEM((FAC_ROWS, 8), I32),
            pltpu.VMEM((2, RATE_ROWS, 128), I32),
            pltpu.VMEM((2, RATE_ROWS, 128), F32),
            pltpu.VMEM(half, F32),
            pltpu.VMEM(half, F32),
            pltpu.VMEM((2, 4) + half, F32),
            pltpu.VMEM((2 * S_ROWS, MAIN), BF),
            pltpu.VMEM((S_ROWS, 128), BF),
            pltpu.VMEM((S_ROWS, 128), F32),
            pltpu.VMEM((TRIOS, TRIO_ROWS, 256), F32),
            pltpu.VMEM((RATE_ROWS, CELLS), BF),
            pltpu.VMEM((RATE_ROWS, CELLS), BF),
            pltpu.VMEM((2, FAC_ROWS, CELLS), BF),
            pltpu.VMEM((2, 16 * PITCH, 128), F32),
            pltpu.VMEM((chunks, BS, BS, 8, 128), F32),
            pltpu.VMEM((chunks, BS, 8, 128), F32),
            pltpu.VMEM((chunks, BS, 8, 128), F32),
            pltpu.VMEM((chunks, BS, 8, 128), F32),
        ],
        compiler_params=pltpu.CompilerParams(
            vmem_limit_bytes=32 * 1024 * 1024, collective_id=0, has_side_effects=True
        ),
        cost_estimate=pl.CostEstimate(
            flops=4_000_000_000, bytes_accessed=3_000_000, transcendentals=400_000
        ),
    )(*args)
    return pl.pallas_call(
        write,
        out_shape=(
            jax.ShapeDtypeStruct((SPEC, CELLS), F32),
            jax.ShapeDtypeStruct((SPEC, 2, FACES), F32),
        ),
        in_specs=[pl.BlockSpec(memory_space=pltpu.VMEM)] * 2,
        out_specs=[pl.BlockSpec(memory_space=pltpu.HBM)] * 2,
        scratch_shapes=[pltpu.SemaphoreType.DMA((3,))],
        compiler_params=pltpu.CompilerParams(vmem_limit_bytes=32 * 1024 * 1024),
    )(advanced, jump)


def solution(mesh):
    cells = P(None, ("grp", "dev"))
    return jax.shard_map(
        on_device,
        mesh=mesh,
        in_specs=(cells, P(("grp", "dev")), P(), P(), P(), P(), cells),
        out_specs=(cells, P(None, None, ("grp", "dev"))),
        check_vma=False,
    )
```

```python
import jax
import jax.numpy as jnp
from jax import lax
from jax.experimental import pallas as pl
from jax.experimental.pallas import tpu as pltpu
from jax.sharding import PartitionSpec as P

NB = 43
BS = 6
RPB = 36
SPEC = 258
NR = 1548
CELLS = 256
FACES = 128

TRIO = 3
TRIOS = 15
TRIO_STATE = TRIO * BS
TRIO_RATES = TRIO * RPB
TRIO_ROWS = 24
JAC_ROWS = BS * TRIO_ROWS
PITCH = JAC_ROWS + 2
LONG = 8 * TRIO_STATE
STATE_ROWS = 2 * LONG + 8
RATE_ROWS = 1552
FAC_ROWS = 1664
S_ROWS = 272
MAIN = 1536
HALF = MAIN // 2
FACE_ROWS = 264
SPREAD = 144
EARLY = 4 * SPREAD

TIME_STEP = 0.01
GAMMA = 0.5
SCALED = TIME_STEP * GAMMA
A = (2.0, 1.867943637803922, 0.2344449711399156)
C = (
    -7.13761503641231,
    2.580708087951457,
    0.6515950076447975,
    -2.137148994382534,
    -0.3214669691237626,
    -0.6949742501781779,
)
M = (2.255570073418735, 0.2870493262186792, 0.435317943184018, 1.093502252409163)

BF = jnp.bfloat16
F32 = jnp.float32
I32 = jnp.int32
MESH = pl.DeviceIdType.MESH

ROW_GATHER = lax.GatherDimensionNumbers(
    offset_dims=(),
    collapsed_slice_dims=(0,),
    start_index_map=(0,),
    operand_batching_dims=(1,),
    start_indices_batching_dims=(1,),
)


LANE_GATHER = lax.GatherDimensionNumbers(
    offset_dims=(),
    collapsed_slice_dims=(1,),
    start_index_map=(1,),
    operand_batching_dims=(0,),
    start_indices_batching_dims=(0,),
)


def dot(a, b):
    return jnp.dot(a, b, preferred_element_type=F32)


def split2(x):
    hi = x.astype(BF)
    return hi, (x - hi.astype(F32)).astype(BF)


def split3(x):
    hi = x.astype(BF)
    rest = x - hi.astype(F32)
    mid = rest.astype(BF)
    return hi, mid, (rest - mid.astype(F32)).astype(BF)


def take_rows(x, index):
    return lax.gather(
        x,
        index[..., None],
        ROW_GATHER,
        slice_sizes=(1, 1),
        mode=lax.GatherScatterMode.PROMISE_IN_BOUNDS,
    )


def take_lanes(x, index):
    return lax.gather(
        x,
        index[..., None],
        LANE_GATHER,
        slice_sizes=(1, 1),
        mode=lax.GatherScatterMode.PROMISE_IN_BOUNDS,
    )


def factor(e):
    for p in range(BS):
        inverse = 1.0 / e[p][p]
        e[p][p] = inverse
        for t in range(p + 1, BS):
            e[t][p] = e[t][p] * inverse
            for c in range(p + 1, BS):
                e[t][c] = e[t][c] - e[t][p] * e[p][c]
    return e


def solve(e, b):
    x = list(b)
    for t in range(BS):
        for c in range(t):
            x[t] = x[t] - e[t][c] * x[c]
    for t in reversed(range(BS)):
        for c in range(t + 1, BS):
            x[t] = x[t] - e[t][c] * x[c]
        x[t] = x[t] * e[t][t]
    return x


def both(a, b):
    return jnp.concatenate([a, b], axis=0)


def lanes(h):
    return slice(h * 128, (h + 1) * 128)


CHUNKS = [(r, s, h) for s in range(2) for h in range(2) for r in range(TRIO)]


def kernel(
    state_hbm,
    flags_hbm,
    reactants_hbm,
    frequency_hbm,
    barrier_hbm,
    stoich_hbm,
    faces_hbm,
    advanced_ref,
    jump_ref,
    state_ref,
    flags_ref,
    reactants_ref,
    frequency_ref,
    barrier_ref,
    stoich_ref,
    faces_ref,
    in_sem,
    face,
    received,
    send_sem,
    recv_sem,
    rows,
    columns,
    whole,
    spots,
    index,
    coef,
    y0,
    y,
    part,
    s_split,
    s_tail,
    tail,
    trio,
    r_hi,
    r_lo,
    fac,
    jac,
    lu,
    u1,
    u2,
    explicit,
):
    me = lax.axis_index("dev")
    count = lax.axis_size("dev")
    up = lax.rem(me + 1, count)
    down = lax.rem(me + count - 1, count)
    loads = [
        pltpu.make_async_copy(src, dst, in_sem.at[k])
        for k, (src, dst) in enumerate(
            [
                (reactants_hbm, reactants_ref),
                (frequency_hbm, frequency_ref),
                (barrier_hbm, barrier_ref),
                (state_hbm, state_ref),
                (stoich_hbm, stoich_ref),
                (flags_hbm, flags_ref),
                (faces_hbm, faces_ref),
            ]
        )
    ]
    for load in loads:
        load.start()

    has_up = me < count - 1
    has_down = me > 0
    barrier = pltpu.get_barrier_semaphore()

    def greet(other):
        pl.semaphore_signal(barrier, inc=1, device_id={"dev": other}, device_id_type=MESH)

    @pl.when(has_up)
    def _():
        greet(up)

    @pl.when(has_down)
    def _():
        greet(down)

    rows[...] = jnp.zeros_like(rows)
    tail[...] = jnp.zeros_like(tail)
    jac[:, TRIOS * PITCH :, :] = jnp.zeros((2, PITCH, 128), F32)
    y0[:, SPEC // 8 * 8 :, :] = jnp.zeros((2, STATE_ROWS - SPEC // 8 * 8, 128), F32)
    part[:, :, :, S_ROWS:, :] = jnp.zeros((2, 4, 2, STATE_ROWS - S_ROWS, 128), F32)
    fac[:, RATE_ROWS:, :] = jnp.zeros((2, FAC_ROWS - RATE_ROWS, CELLS), BF)
    for load in loads[:3]:
        load.wait()

    reactants = reactants_ref[...]
    first = ((lax.broadcasted_iota(I32, (2, NR), 1) * 1821) >> 16) * BS
    for k, ref in ((0, frequency_ref), (3, barrier_ref)):
        for q, piece in enumerate(split3(ref[...].reshape(1, NR))):
            rows[k + q : k + q + 1, :NR] = piece.astype(F32)
    whole[...] = jnp.zeros_like(whole)
    whole[0:2, :NR] = reactants
    whole[2:4, :NR] = reactants - first
    spots[...] = jnp.transpose(whole[...])
    columns[...] = jnp.transpose(rows[...]).astype(BF)
    row = lax.broadcasted_iota(I32, (8, 256), 0)
    col = lax.broadcasted_iota(I32, (8, 256), 1)
    pick = ((row >= 3) == (col >= 128)).astype(F32).astype(BF)
    loads[3].wait()

    for h in range(2):
        y0[h, :SPEC, :] = state_ref[:, lanes(h)]

    sub = lax.broadcasted_iota(I32, (8, 128), 0)

    def reactant(ref, h, at, want):
        one = at // RPB
        two = min((at + 7) // RPB, NB - 1)
        got = take_rows(ref[h, one * BS : one * BS + 8, :], want)
        if two != one:
            other = take_rows(ref[h, two * BS : two * BS + 8, :], want)
            got = jnp.where(sub < two * RPB - at, got, other)
        return got

    def put_rates(at, h, values):
        hi, lo = split2(both(*values))
        r_hi[at : at + 16, lanes(h)] = hi
        r_lo[at : at + 16, lanes(h)] = lo

    theta = 1.0 - 1.0 / state_ref[SPEC - 1 : SPEC, :]
    def begin(at, wide):
        wants, freq, ener = [], [], []
        for k in (at, at + 8):
            own = wide[k % SPREAD : k % SPREAD + 8, :]
            freq.append(own[:, :128])
            ener.append(own[:, 128:256])
            want = [
                jnp.broadcast_to(spots[k : k + 8, 2 + w : 3 + w], (8, 128)) for w in range(2)
            ]
            for w in range(2):
                index[w, k : k + 8, :] = want[w] - sub
            wants.append(want)
        for h in range(2):
            one, two, rate = [], [], []
            for q, k in enumerate((at, at + 8)):
                c = freq[q] * jnp.exp(ener[q] * theta[:, lanes(h)])
                coef[h, k : k + 8, :] = c
                former = reactant(y0, h, k, wants[q][0])
                latter = reactant(y0, h, k, wants[q][1])
                one.append(c * latter)
                two.append(c * former)
                rate.append(one[-1] * former)
            fac[0, at : at + 16, lanes(h)] = both(*one).astype(BF)
            fac[1, at : at + 16, lanes(h)] = both(*two).astype(BF)
            put_rates(at, h, rate)

    def split_stoichiometry(k):
        span = slice(k * HALF, (k + 1) * HALF)
        for at in range(0, SPEC, 16):
            n = min(16, SPEC - at)
            x = stoich_ref[at : at + n, span]
            if n < 16:
                x = both(x, jnp.zeros((16 - n, HALF), F32))
            hi, lo = split2(x)
            s_split[at : at + 16, span] = hi
            s_split[S_ROWS + at : S_ROWS + at + 16, span] = lo

    def split_tail():
        tail[:SPEC, : NR - MAIN] = stoich_ref[:, MAIN:]
        for at in range(0, S_ROWS, 16):
            x = tail[at : at + 16, :]
            hi = x.astype(BF).astype(F32)
            lo = x - hi
            s_tail[at : at + 16, :] = (
                hi + pltpu.roll(lo, 16, 1) + pltpu.roll(hi, 32, 1)
            ).astype(BF)

    def source_part(stage, k, top=0, end=S_ROWS):
        low, mid, near, high = (k * HALF + q for q in (0, 512, 256, 768))
        n = end - top

        def stacked(span):
            hi = s_split[top:end, span]
            lo = s_split[S_ROWS + top : S_ROWS + end, span]
            long = dot(both(hi, lo), r_hi[span, :])
            return long[:n] + long[n:]

        def corrected(span):
            return dot(s_split[top:end, span], r_lo[span, :])

        one = stacked(slice(low, mid)) + corrected(slice(low, near))
        two = stacked(slice(mid, high)) + corrected(slice(near, high))
        if k == 1:
            last = jnp.concatenate([r_hi[MAIN:, :], r_hi[MAIN:, :], r_lo[MAIN:, :]], axis=0)
            two = two + dot(s_tail[top:end, :48], last)
        for q, total in enumerate((one, two)):
            for h in range(2):
                part[stage % 2, 2 * k + q, h, top:end, :] = total[:, lanes(h)]

    def again(at):
        wants = [[index[w, k : k + 8, :] + sub for w in range(2)] for k in (at, at + 8)]
        for h in range(2):
            put_rates(
                at,
                h,
                [
                    coef[h, k : k + 8, :] * reactant(y, h, k, want[0]) * reactant(y, h, k, want[1])
                    for k, want in zip((at, at + 8), wants)
                ],
            )

    def state_rows(r, s, m):
        return pl.ds(s * LONG + r * BS + m, 8, stride=TRIO_STATE)

    def spread(ref, r, s, h):
        return [ref[h, state_rows(r, s, m), :] for m in range(BS)]

    def source(stage, r, s, h):
        own = part.at[stage % 2]
        return [
            (own[0, h, state_rows(r, s, m), :] + own[1, h, state_rows(r, s, m), :])
            + (own[2, h, state_rows(r, s, m), :] + own[3, h, state_rows(r, s, m), :])
            for m in range(BS)
        ]

    def put_state(ref, r, s, h, values):
        for m in range(BS):
            ref[h, state_rows(r, s, m), :] = values[m]

    def keep(ref, k, values):
        for m in range(BS):
            ref[k, m] = values[m]

    def kept(ref, k):
        return [ref[k, m] for m in range(BS)]

    def factors(k):
        return [[lu[k, i, m] for m in range(BS)] for i in range(BS)]

    shift = ((lax.broadcasted_iota(I32, (TRIO_ROWS, 1), 0) * 43) >> 8) * BS
    def jacobian(t):
        start = t * TRIO_RATES // 16 * 16
        low = start // 128 * 128
        top = t * TRIO_STATE
        n = min(TRIO_STATE, SPEC - top)
        wide = min(256, NR - low)
        if wide < 256 or n < TRIO_STATE:
            trio[t] = jnp.zeros((TRIO_ROWS, 256), F32)
        trio[t, :n, :wide] = stoich_ref[top : top + n, low : low + wide] * -SCALED
        x = trio[t]
        reacts = whole[:, low : low + 256]
        if start > low:
            x = pltpu.roll(x, 256 - (start - low), 1)
            reacts = pltpu.roll(reacts, 256 - (start - low), 1)
        x = x[:, :128]
        reacts = reacts[:, :128]
        sides = []
        for w in range(2):
            where = reacts[w : w + 1, :] - (shift + top)
            sides.append(
                jnp.concatenate([jnp.where(where == m, x, 0.0) for m in range(BS)], axis=0)
            )
        coupling = jnp.concatenate([side.astype(BF) for side in sides], axis=1)
        factors_here = both(fac[0, start : start + 128, :], fac[1, start : start + 128, :])
        block = dot(coupling, factors_here)
        for h in range(2):
            jac[h, t * PITCH : t * PITCH + JAC_ROWS, :] = block[:, lanes(h)]

    def eliminate(s):
        for k, (r, s_k, h) in enumerate(CHUNKS):
            if s_k != s:
                continue
            e = [
                [
                    jac[h, pl.ds(s * 8 * PITCH + m * TRIO_ROWS + r * BS + i, 8, stride=PITCH), :]
                    for m in range(BS)
                ]
                for i in range(BS)
            ]
            for i in range(BS):
                e[i][i] = 1.0 + e[i][i]
            e = factor(e)
            for i in range(BS):
                for m in range(BS):
                    lu[k, i, m] = e[i][m]

    def first_stage(k, r, s, h):
        rhs = source(0, r, s, h)
        x = solve(factors(k), rhs)
        start = spread(y0, r, s, h)
        keep(u1, k, x)
        keep(explicit, k, [a + TIME_STEP * b for a, b in zip(start, rhs)])
        put_state(y, r, s, h, [a + (SCALED * A[0]) * b for a, b in zip(start, x)])

    def second_stage(k, r, s, h):
        one = kept(u1, k)
        x = solve(factors(k), [a + (GAMMA * C[0]) * b for a, b in zip(source(1, r, s, h), one)])
        keep(u2, k, x)
        put_state(
            y,
            r,
            s,
            h,
            [
                a + (SCALED * A[1]) * b + (SCALED * A[2]) * c
                for a, b, c in zip(spread(y0, r, s, h), one, x)
            ],
        )

    def next_source(stage, step):
        for half in range(2):
            for k, (r, s, h) in enumerate(CHUNKS):
                if s == half:
                    step(k, r, s, h)
            for at in range(half * HALF, HALF if half == 0 else RATE_ROWS, 16):
                again(at)
            if stage == 2 and half == 1:
                source_part(stage, half, 0, LONG)
            else:
                source_part(stage, half)

    for at in range(0, RATE_ROWS, 16):
        if at % SPREAD == 0:
            wide = dot(columns[at : min(at + SPREAD, RATE_ROWS), :], pick)
        if at == EARLY:
            for load in loads[4:]:
                load.wait()
        begin(at, wide)
        if at + 16 == HALF:
            split_stoichiometry(0)
            source_part(0, 0)
    split_stoichiometry(1)
    split_tail()
    for t in range(8):
        jacobian(t)
    source_part(0, 1)
    for t in range(8, TRIOS):
        jacobian(t)
    eliminate(0)
    eliminate(1)

    next_source(1, first_stage)
    next_source(2, second_stage)

    cells = [jnp.broadcast_to(faces_ref[r : r + 1, :], (8, FACES)) for r in range(2)]
    near = [c < 128 for c in cells]
    cells = [c & 127 for c in cells]

    def neighbour(r, s, other):
        here = pl.ds(s * LONG, LONG if s == 0 else SPEC - LONG)
        return pltpu.make_async_remote_copy(
            src_ref=face.at[r, here],
            dst_ref=received.at[1 - r, here],
            send_sem=send_sem.at[r, s],
            recv_sem=recv_sem.at[1 - r, s],
            device_id={"dev": other},
            device_id_type=MESH,
        )

    for s in range(2):
        if s == 1:
            source_part(2, 1, LONG, S_ROWS)
        for k, (r, s_k, h) in enumerate(CHUNKS):
            if s_k != s:
                continue
            e = factors(k)
            one = kept(u1, k)
            two = kept(u2, k)
            base = source(2, r, s, h)
            three = solve(
                e,
                [
                    z + (GAMMA * C[1]) * a + (GAMMA * C[2]) * b
                    for z, a, b in zip(base, one, two)
                ],
            )
            rest = solve(
                e,
                [
                    (M[2] + M[3]) * z
                    + (GAMMA * (M[2] * C[1] + M[3] * C[3])) * a
                    + (GAMMA * (M[2] * C[2] + M[3] * C[4])) * b
                    + (GAMMA * M[3] * C[5]) * c
                    for z, a, b, c in zip(base, one, two, three)
                ],
            )
            stiff = flags_ref[lanes(h)].reshape(1, 128) == 1
            put_state(
                y,
                r,
                s,
                h,
                [
                    jnp.where(
                        stiff,
                        z + (SCALED * M[0]) * a + (SCALED * M[1]) * b + SCALED * d,
                        x,
                    )
                    for z, a, b, d, x in zip(
                        spread(y0, r, s, h), one, two, rest, kept(explicit, k)
                    )
                ],
            )
        here = slice(s * LONG, (s + 1) * LONG)
        n = min(LONG, SPEC - s * LONG)
        done = jnp.concatenate([y[0, here, :], y[1, here, :]], axis=1)
        advanced_ref[s * LONG : s * LONG + n, :] = done[:n]
        for at in range(s * LONG, LONG if s == 0 else FACE_ROWS, 8):
            halves = [y[h, at : at + 8, :] for h in range(2)]
            for r in range(2):
                face[r, at : at + 8, :] = jnp.where(
                    near[r], take_lanes(halves[0], cells[r]), take_lanes(halves[1], cells[r])
                )

        if s == 0:
            pl.semaphore_wait(barrier, has_up.astype(I32) + has_down.astype(I32))

        @pl.when(has_down)
        def _(s=s):
            neighbour(0, s, down).start()

        @pl.when(has_up)
        def _(s=s):
            neighbour(1, s, up).start()

    for r, there, other in ((0, has_down, down), (1, has_up, up)):

        @pl.when(there)
        def _(r=r, other=other):
            for s in range(2):
                neighbour(1 - r, s, other).wait_recv()
                n = min(SPEC - s * LONG, LONG)
                here = slice(s * LONG, s * LONG + n)
                jump_ref[r, here, :] = received[r, here, :] - face[r, here, :]
            for s in range(2):
                neighbour(r, s, other).wait_send()

        @pl.when(jnp.logical_not(there))
        def _(r=r):
            jump_ref[r] = 0.0 - face[r, :SPEC, :]


def write(advanced, jump, advanced_hbm, jump_hbm, sem):
    copies = [
        pltpu.make_async_copy(advanced, advanced_hbm, sem.at[0]),
        pltpu.make_async_copy(jump.at[0], jump_hbm.at[:, 0, :], sem.at[1]),
        pltpu.make_async_copy(jump.at[1], jump_hbm.at[:, 1, :], sem.at[2]),
    ]
    for copy in copies:
        copy.start()
    for copy in copies:
        copy.wait()


def on_device(*args):
    args = [pltpu.with_memory_space_constraint(x, pltpu.HBM) for x in args]
    half = (2, STATE_ROWS, 128)
    chunks = len(CHUNKS)
    advanced, jump = pl.pallas_call(
        kernel,
        out_shape=(
            jax.ShapeDtypeStruct((SPEC, CELLS), F32),
            jax.ShapeDtypeStruct((2, SPEC, FACES), F32),
        ),
        in_specs=[pl.BlockSpec(memory_space=pltpu.HBM)] * 7,
        out_specs=[pl.BlockSpec(memory_space=pltpu.VMEM)] * 2,
        scratch_shapes=[
            pltpu.VMEM((SPEC, CELLS), F32),
            pltpu.VMEM((CELLS,), I32),
            pltpu.VMEM((2, NR), I32),
            pltpu.VMEM((NR,), F32),
            pltpu.VMEM((NR,), F32),
            pltpu.VMEM((SPEC, NR), F32),
            pltpu.VMEM((2, FACES), I32),
            pltpu.SemaphoreType.DMA((7,)),
            pltpu.VMEM((2, FACE_ROWS, FACES), F32),
            pltpu.VMEM((2, FACE_ROWS, FACES), F32),
            pltpu.SemaphoreType.DMA((2, 2)),
            pltpu.SemaphoreType.DMA((2, 2)),
            pltpu.VMEM((8, FAC_ROWS), F32),
            pltpu.VMEM((FAC_ROWS, 8), BF),
            pltpu.VMEM((8, FAC_ROWS), I32),
            pltpu.VMEM((FAC_ROWS, 8), I32),
            pltpu.VMEM((2, RATE_ROWS, 128), I32),
            pltpu.VMEM((2, RATE_ROWS, 128), F32),
            pltpu.VMEM(half, F32),
            pltpu.VMEM(half, F32),
            pltpu.VMEM((2, 4) + half, F32),
            pltpu.VMEM((2 * S_ROWS, MAIN), BF),
            pltpu.VMEM((S_ROWS, 128), BF),
            pltpu.VMEM((S_ROWS, 128), F32),
            pltpu.VMEM((TRIOS, TRIO_ROWS, 256), F32),
            pltpu.VMEM((RATE_ROWS, CELLS), BF),
            pltpu.VMEM((RATE_ROWS, CELLS), BF),
            pltpu.VMEM((2, FAC_ROWS, CELLS), BF),
            pltpu.VMEM((2, 16 * PITCH, 128), F32),
            pltpu.VMEM((chunks, BS, BS, 8, 128), F32),
            pltpu.VMEM((chunks, BS, 8, 128), F32),
            pltpu.VMEM((chunks, BS, 8, 128), F32),
            pltpu.VMEM((chunks, BS, 8, 128), F32),
        ],
        compiler_params=pltpu.CompilerParams(
            vmem_limit_bytes=32 * 1024 * 1024, collective_id=0, has_side_effects=True
        ),
        cost_estimate=pl.CostEstimate(
            flops=4_000_000_000, bytes_accessed=3_000_000, transcendentals=400_000
        ),
    )(*args)
    return pl.pallas_call(
        write,
        out_shape=(
            jax.ShapeDtypeStruct((SPEC, CELLS), F32),
            jax.ShapeDtypeStruct((SPEC, 2, FACES), F32),
        ),
        in_specs=[pl.BlockSpec(memory_space=pltpu.VMEM)] * 2,
        out_specs=[pl.BlockSpec(memory_space=pltpu.HBM)] * 2,
        scratch_shapes=[pltpu.SemaphoreType.DMA((3,))],
        compiler_params=pltpu.CompilerParams(vmem_limit_bytes=32 * 1024 * 1024),
    )(advanced, jump)


def solution(mesh):
    cells = P(None, ("grp", "dev"))
    return jax.shard_map(
        on_device,
        mesh=mesh,
        in_specs=(cells, P(("grp", "dev")), P(), P(), P(), P(), cells),
        out_specs=(cells, P(None, None, ("grp", "dev"))),
        check_vma=False,
    )
```
